128 devices in a mesh: leaf: 64 (over z, x, y), grp: 2 (over core).
Axes of the slice: x: 4, y: 4, z: 4, core: 2. Of those that a mesh axis runs over, the one named last changes fastest.
Arguments:
- positions: float32 [3, 65536, 256], P(None, ('leaf', 'grp')), may hold values from 0 to 1
- charges: float32 [65536, 256], P(('leaf', 'grp')), may hold values from -0.12 to 0.12
- counts: int32 [65536], P(('leaf', 'grp')), may hold values from 96 to 256, as said below
- send_left: int32 [32768], P(('leaf', 'grp')), may hold values from 0 to 511, as said below
- pairs: int32 [3, 114688], P(None, ('leaf', 'grp')), may hold values from 0 to 767, as said below
Outputs:
- fields: float32 [4, 65536, 256], P(None, ('leaf', 'grp'))
The draws below stay inside these ranges and needn't reach their ends.
Inputs may be any that keep to these rules, and one draw needn't show every extreme that they name: `counts`: each leaf holds at least 96 particles and in every device some leaf is full. `send_left`: within each device's 256 entries the indices are distinct. Each device's 896 columns are, in order: 512 self pairs (a, a, 13) of its leaves; 128 pairs of two different local leaves with a code other than 13; 256 pairs whose first leaf is a local leaf and whose second is 512 + k, naming the next device's k-th send_left leaf, with a code other than 13.
All inputs are finite; a program needn't handle non-finite values.
Results may differ from the reference program's by a relative error of at most 0.0003.
Values sent between devices are 32-bit elements; how exact they have to be, the bound alone decides.
A program may use at most 64 MiB of HBM per device.

```python
import jax
import jax.numpy as jnp
from jax import lax

LD = 512
SLOTS = 256
SB = 256
PD = 896
LEAVES = 65536


def draw_send_left(key, part):
    key = jax.random.fold_in(key, 5)
    devices = LEAVES // LD
    keys = jax.random.split(key, devices)
    first = jax.vmap(lambda device_key: jax.random.permutation(device_key, LD)[:SB])(keys)
    return first.reshape(-1).astype(jnp.int32)


def draw_counts(key, part):
    key = jax.random.fold_in(key, 7)
    devices = LEAVES // LD
    key_one, key_two = jax.random.split(key)
    filled = jax.random.randint(key_one, (devices, LD), 96, SLOTS + 1)
    chosen = jax.random.randint(key_two, (devices, 1), 0, LD)
    filled = jnp.where(jnp.arange(LD)[None, :] == chosen, SLOTS, filled)
    return filled.reshape(-1).astype(jnp.int32)


def draw_pairs(key, part):
    key = jax.random.fold_in(key, 3)
    devices = LEAVES // LD
    local_count = LD // 4
    cross_count = LD // 2
    keys = jax.random.split(key, 6)

    def codes(code_key, shape):
        raw = jax.random.randint(code_key, shape, 0, 26)
        return raw + (raw >= 13).astype(jnp.int32)
    self_leaf = jnp.broadcast_to(jnp.arange(LD, dtype=jnp.int32)[None, :], (devices, LD))
    local_first = jax.random.randint(keys[0], (devices, local_count), 0, LD)
    local_second = (local_first + jax.random.randint(keys[1], (devices, local_count), 1, LD)) % LD
    cross_first = jax.random.randint(keys[2], (devices, cross_count), 0, LD)
    cross_second = LD + jax.random.randint(keys[3], (devices, cross_count), 0, SB)
    last_col = jnp.arange(cross_count)[None, :] == cross_count - 1
    cross_second = jnp.where(last_col, LD + SB - 1, cross_second)
    cross_codes = jnp.where(last_col, 26, codes(keys[5], (devices, cross_count)))
    first_col = jnp.concatenate([self_leaf, local_first, cross_first], 1)
    second_col = jnp.concatenate([self_leaf, local_second, cross_second], 1)
    code_col = jnp.concatenate([jnp.full((devices, LD), 13, jnp.int32), codes(keys[4], (devices, local_count)), cross_codes], 1)
    return jnp.stack([first_col, second_col, code_col]).reshape(3, -1).astype(jnp.int32)


def steps_of(stream_key, dims, pieces, least, largest):
    level = 1.0
    for position, parts in pieces:
        draws = jax.random.uniform(jax.random.fold_in(jax.random.fold_in(stream_key, 6), position), (parts,), jnp.float32, least / len(pieces), largest / len(pieces))
        level = level * jnp.repeat(jnp.exp(draws), dims[position] // parts).reshape((-1,) + (1,) * (len(dims) - 1 - position))
    return level


def centred(key, dims, scale, reach, cuts=(), held_as=jnp.bfloat16):
    factor_of = steps_of(key, dims, cuts, -0.22, 0.18) if cuts else 1.0
    values = jax.random.normal(key, dims, jnp.float32) * scale * factor_of
    return jnp.minimum(jnp.maximum(values, -reach), reach).astype(held_as)


def setup_inputs(seed: int = 0) -> dict:
    streams_of = jax.random.split(jax.random.key(seed), 6)
    return {
        "positions": jnp.clip(1.0 * jax.random.uniform(streams_of[0], (3, LEAVES, SLOTS), jnp.float32) ** steps_of(streams_of[0], (3, LEAVES, SLOTS), ((1, 128),), -0.2, 0.2), 0.0, 1.0),
        "charges": centred(streams_of[1], (LEAVES, SLOTS), 0.02, 0.12, ((0, 128),), jnp.float32),
        "counts": draw_counts(jax.random.fold_in(streams_of[5], 71), 0),
        "send_left": draw_send_left(jax.random.fold_in(streams_of[5], 71), 0),
        "pairs": draw_pairs(jax.random.fold_in(streams_of[5], 71), 0),
    }


SOFTEN = 0.05

def offsets(code):
    return jnp.stack([code // 9 - 1, code // 3 % 3 - 1, code % 3 - 1]).astype(jnp.float32)

def pair_terms(target, source, displace, coincide, first_slot):
    slots_t = target.shape[2]
    slots_s = source.shape[2]
    diff = target[:3, :, :, None] - (source[:3, :, None, :] + displace[:, :, None, None])
    radius2 = lax.optimization_barrier(jnp.sum(diff * diff, axis=0)) + SOFTEN
    diagonal = (jnp.arange(slots_t)[:, None] + first_slot == jnp.arange(slots_s)[None, :]).astype(jnp.float32)
    weight = 1.0 / jnp.sqrt(radius2) * (1.0 - coincide[:, None, None] * diagonal[None])
    cubed = weight * weight * weight
    charge_s = source[3][:, None, :]
    charge_t = target[3][:, :, None]
    phi_t = lax.optimization_barrier(jnp.sum(weight * charge_s, axis=2))
    field_t = lax.optimization_barrier(jnp.sum(diff * (cubed * charge_s)[None], axis=3))
    phi_s = lax.optimization_barrier(jnp.sum(weight * charge_t, axis=1))
    field_s = -lax.optimization_barrier(jnp.sum(diff * (cubed * charge_t)[None], axis=2))
    return (jnp.concatenate([phi_t[None], field_t], 0), jnp.concatenate([phi_s[None], field_s], 0))

def accumulate(pool, pair_rows):
    block = LD // 16
    blocks = pair_rows.shape[1] // block
    rows = pair_rows.reshape(3, blocks, block)

    def step(totals, inputs):
        first_leaf, second_leaf, kind = inputs
        target = jnp.take(pool, first_leaf, axis=1)
        source = jnp.take(pool, second_leaf, axis=1)
        coincide = (first_leaf == second_leaf).astype(jnp.float32)
        on_target, on_source = pair_terms(target, source, offsets(kind), coincide, 0)
        totals = totals.at[:, first_leaf].add(on_target)
        totals = totals.at[:, second_leaf].add(on_source * (1.0 - coincide)[None, :, None])
        return (totals, None)
    totals, unused = lax.scan(step, jnp.zeros(pool.shape, jnp.float32), (rows[0], rows[1], rows[2]))
    return totals

def reference(positions, charges, counts, send_left, pairs):
    devices = LEAVES // LD
    occupied = (jnp.arange(SLOTS)[None, :] < counts[:, None]).astype(jnp.float32)
    sources = jnp.concatenate([positions, (charges * occupied)[None]], 0)
    sources = sources.reshape(4, devices, LD, SLOTS).transpose(1, 0, 2, 3)
    left_lists = send_left.reshape(devices, SB)
    outgoing = jax.vmap(lambda whole, chosen: jnp.take(whole, chosen, axis=1))(sources, left_lists)
    remote = jnp.concatenate([outgoing[1:], jnp.zeros_like(outgoing[:1])], 0)
    pools = jnp.concatenate([sources, remote], 2)
    pair_sets = pairs.reshape(3, devices, PD).transpose(1, 0, 2)
    totals = lax.map(lambda packed: accumulate(packed[0], packed[1]), (pools, pair_sets))
    own = totals[:, :, :LD]
    returned = totals[:, :, LD:]
    arriving = jnp.concatenate([jnp.zeros_like(returned[:1]), returned[:-1]], 0)
    own = jax.vmap(lambda mine, extra, chosen: mine.at[:, chosen].add(extra))(own, arriving, left_lists)
    fields = own.transpose(1, 0, 2, 3).reshape(4, LEAVES, SLOTS)
    return fields * occupied[None]
```

```python
import functools
import numpy as np
import jax, jax.numpy as jnp
from jax import lax
from jax.experimental import pallas as pl
from jax.experimental.pallas import tpu as pltpu
from jax.sharding import PartitionSpec as P

F32 = jnp.float32
BF16 = jnp.bfloat16
SOFTEN = 0.05
CELL = 128
NN = (((1,), (0,)), ((), ()))
TN = (((0,), (0,)), ((), ()))


def offset_tables():
    code = np.arange(27)
    o = np.stack([code // 9 - 1, code // 3 % 3 - 1, code % 3 - 1], 1).astype(np.float32)
    scale = np.zeros((27, 16), np.float32)
    scale[:, 0:3] = 2 * o
    scale[:, 8:11] = 2 * o
    const = np.zeros((27, 16), np.float32)
    const[:, 3] = (o * o).sum(1)
    const[:, 4:7] = o
    const[:, 7] = 1
    const[:, 11] = 1
    const[:, 12:15] = o
    shift = np.zeros((27, 16), np.float32)
    shift[:, 0:3] = o
    shift[:, 4:7] = o * o
    shift[:, 12:15] = 2 * o
    wide = lambda t: np.broadcast_to(t[:, :, None], (27, 16, CELL))
    return jnp.asarray(wide(scale), BF16), jnp.asarray(wide(const), BF16), jnp.asarray(wide(shift), F32)


def rounded(x):
    return x.astype(BF16).astype(F32)


def two_parts(x):
    high = rounded(x)
    return high, rounded(x - high)


def three_parts(x):
    high, middle = two_parts(x)
    return high, middle, x - high - middle


def features(pos, q, rows_r, rows_q, rows_l):
    highs, mids, coords = [], [], []
    for x in pos:
        high, mid = two_parts(x - 0.5)
        highs.append(high)
        mids.append(mid)
        coords.append(high + mid)
    squares = [c * c for c in coords]
    norm = squares[0] + squares[1] + squares[2]
    s = three_parts(norm)
    for i in range(3):
        for base in (0, 4):
            rows_r[pl.ds(base + i, 8, stride=16), :] = highs[i]
            rows_r[pl.ds(8 + base + i, 8, stride=16), :] = mids[i]
    one = jnp.ones_like(q)
    rows_r[pl.ds(3, 8, stride=16), :] = one
    rows_r[pl.ds(7, 8, stride=16), :] = s[0]
    rows_r[pl.ds(11, 8, stride=16), :] = s[2]
    rows_r[pl.ds(15, 8, stride=16), :] = s[1]
    for i in range(3):
        for row, value in ((i, coords[i]), (4 + i, squares[i])):
            high, mid = two_parts(q * value)
            rows_q[pl.ds(row, 8, stride=16), :] = high
            rows_q[pl.ds(8 + row, 8, stride=16), :] = mid
    high, mid = two_parts(q)
    rows_q[pl.ds(3, 8, stride=16), :] = high
    rows_q[pl.ds(11, 8, stride=16), :] = mid
    if rows_l is not None:
        n = three_parts(norm + SOFTEN)
        for i in range(3):
            h, m = -2.0 * highs[i], -2.0 * mids[i]
            rows_l[pl.ds(i, 8, stride=32), :] = h
            rows_l[pl.ds(4 + i, 8, stride=32), :] = m
            rows_l[pl.ds(8 + i, 8, stride=32), :] = h
            rows_l[pl.ds(12 + i, 8, stride=32), :] = m
            rows_l[pl.ds(20 + i, 8, stride=32), :] = h
            rows_l[pl.ds(28 + i, 8, stride=32), :] = m
        rows_l[pl.ds(3, 8, stride=32), :] = n[0]
        rows_l[pl.ds(23, 8, stride=32), :] = n[1]
        rows_l[pl.ds(27, 8, stride=32), :] = n[2]


def prepare(pos_at, q_at, leaves, slots, stage_r, stage_q, stage_l, R, Q, L):
    halves = slots // CELL
    for h in range(halves):
        stage_q[h, pl.ds(7, 8, stride=16), :] = jnp.zeros((8, CELL), F32)
        stage_q[h, pl.ds(15, 8, stride=16), :] = jnp.zeros((8, CELL), F32)
        if L is not None:
            for row in (7, 11, 15, 16, 17, 18, 19, 24, 25, 26):
                stage_l[h, pl.ds(row, 8, stride=32), :] = jnp.ones((8, CELL), F32)
            stage_l[h, pl.ds(31, 8, stride=32), :] = jnp.zeros((8, CELL), F32)

    @pl.loop(0, leaves // 8)
    def _(g):
        first = pl.multiple_of(g * 8, 8)
        for h in range(halves):
            lanes = slice(h * CELL, (h + 1) * CELL)
            pos = [pos_at(i, pl.ds(first, 8), lanes) for i in range(3)]
            q = q_at(pl.ds(first, 8), lanes)
            features(pos, q, stage_r.at[h], stage_q.at[h], None if L is None else stage_l.at[h])
            to = pl.ds(h * leaves + first, 8)
            R[to] = stage_r[h].reshape(8, 16, CELL).astype(BF16)
            Q[to] = stage_q[h].reshape(8, 16, CELL).astype(BF16)
            if L is not None:
                L[to] = stage_l[h].reshape(8, 32, CELL).astype(BF16)


def cell_loop(U, items, batches, scale, const, shift, L, Qa, acc_a, R, Qb, acc_b, gram, weights, turned, both):
    def decode(i):
        e = items[i]
        return e & 2047, (e >> 11) & 2047, e >> 22

    def add(acc, at, q, w, code):
        out = lax.dot_general(jnp.concatenate([q, q], 1), w, NN, preferred_element_type=F32)
        m = out[0:8] + out[8:16]
        if both:
            a = jnp.broadcast_to(m[3:4], m.shape)
            m = m + shift[code, 0:8] * a + shift[code, 8:16] * pltpu.roll(m, 4, 0)
        acc[at] += m

    @pl.loop(0, batches + 3)
    def _(j):
        if both:
            for k in range(U):
                a, b, code = decode(j * U + k)
                add(acc_a, a, Qb[b], turned[k], code)
        for k in range(U):
            a, b, code = decode((j + 1) * U + k)
            w = weights[k]
            if both:
                add(acc_b, b, Qa[a], w, 26 - code)
                turned[k, 0:CELL] = w[0:CELL].T
                turned[k, CELL:] = w[CELL:].T
            else:
                add(acc_a, a, Qb[b], w, code)
        for k in range(U):
            w = lax.rsqrt(gram[k])
            w3 = w * w * w
            high = w3.astype(BF16)
            weights[k, 0:CELL] = high
            weights[k, CELL:] = (w3 - high.astype(F32)).astype(BF16)
        for k in range(U):
            a, b, code = decode((j + 3) * U + k)
            r0 = R[b]
            r1 = r0 * scale[code] + const[code]
            gram[k] = lax.dot_general(L[a], jnp.concatenate([r0, r1], 0), TN, preferred_element_type=F32)


def batches_of(n, U):
    return lax.div(n + U - 1, U)


def idle(dummy_a, dummy_b):
    return dummy_a + dummy_b * 2048 + 13 * (1 << 22)


def fill(items, start, n, value):
    @pl.loop(0, n)
    def _(i):
        items[start + i] = value


def local_kernel(U, leaves, slots, npairs, pos, q, counts, pairs, scale, const, shift, acc, L, Q, R, stage_r, stage_q,
                 stage_l, diag, cross, gram, weights, turned):
    dummy = 2 * leaves
    acc[...] = jnp.zeros_like(acc)
    R[dummy] = jnp.zeros(R.shape[1:], BF16)
    Q[dummy] = jnp.zeros(Q.shape[1:], BF16)
    L[dummy] = jnp.ones(L.shape[1:], BF16)
    gram[...] = jnp.ones_like(gram)
    weights[...] = jnp.zeros_like(weights)
    turned[...] = jnp.zeros_like(turned)
    none = idle(dummy, dummy)
    for k in range(3 * U):
        diag[k] = none
        cross[k] = none
    prepare(lambda i, r, s: pos[i, r, s], lambda r, s: q[r, s], leaves, slots, stage_r, stage_q, stage_l, R, Q, L)
    code0 = 13 * (1 << 22)

    def own(l, carry):
        nd, nx = carry
        more = (counts[l] > CELL).astype(jnp.int32)
        diag[nd] = l * 2049 + code0
        diag[nd + 1] = (l + leaves) * 2049 + code0
        cross[nx] = l + (l + leaves) * 2048 + code0
        return nd + 1 + more, nx + more

    nd, nx = lax.fori_loop(0, leaves, own, (3 * U, 3 * U), unroll=8)

    def near(i, nx):
        a, b, code = pairs[0, i], pairs[1, i], pairs[2, i]
        more_a = (counts[a] > CELL).astype(jnp.int32)
        more_b = (counts[b] > CELL).astype(jnp.int32)
        e = a + b * 2048 + code * (1 << 22)
        cross[nx] = e
        nx += 1
        cross[nx] = e + leaves
        nx += more_a
        cross[nx] = e + leaves * 2048
        nx += more_b
        cross[nx] = e + leaves * 2049
        return nx + more_a * more_b

    nx = lax.fori_loop(leaves, leaves + npairs, near, nx, unroll=4)
    fill(diag, nd, 5 * U, none)
    fill(cross, nx, 5 * U, none)
    loop = functools.partial(cell_loop, U)
    loop(diag, batches_of(nd - 3 * U, U), scale, const, shift, L, Q, acc, R, Q, acc, gram, weights, turned, False)
    weights[...] = jnp.zeros_like(weights)
    loop(cross, batches_of(nx - 3 * U, U), scale, const, shift, L, Q, acc, R, Q, acc, gram, weights, turned, True)


def remote_kernel(U, leaves, remotes, slots, npairs, first, rpos, counts, rcounts, pairs, scale, const, shift, L, Qa,
                  acc_in, acc, back, R, Q, acc_b, stage_r, stage_q, cross, gram, weights, turned):
    dummy_a, dummy_b = 2 * leaves, 2 * remotes
    acc[...] = acc_in[...]
    acc_b[...] = jnp.zeros_like(acc_b)
    R[dummy_b] = jnp.zeros(R.shape[1:], BF16)
    Q[dummy_b] = jnp.zeros(Q.shape[1:], BF16)
    gram[...] = jnp.ones_like(gram)
    weights[...] = jnp.zeros_like(weights)
    turned[...] = jnp.zeros_like(turned)
    none = idle(dummy_a, dummy_b)
    for k in range(3 * U):
        cross[k] = none
    prepare(lambda i, r, s: rpos[i, r, s], lambda r, s: rpos[3, r, s], remotes, slots, stage_r, stage_q, None, R, Q, None)

    def far(i, nx):
        a, b, code = pairs[0, i], pairs[1, i] - leaves, pairs[2, i]
        more_a = (counts[a] > CELL).astype(jnp.int32)
        more_b = (rcounts[b] > CELL).astype(jnp.int32)
        e = a + b * 2048 + code * (1 << 22)
        cross[nx] = e
        nx += 1
        cross[nx] = e + leaves
        nx += more_a
        cross[nx] = e + remotes * 2048
        nx += more_b
        cross[nx] = e + remotes * 2048 + leaves
        return nx + more_a * more_b

    nx = lax.fori_loop(first, first + npairs, far, 3 * U, unroll=4)
    fill(cross, nx, 5 * U, none)
    cell_loop(U, cross, batches_of(nx - 3 * U, U), scale, const, shift, L, Qa, acc, R, Q, acc_b, gram, weights, turned, True)

    @pl.loop(0, remotes // 8)
    def _(g):
        r = pl.ds(pl.multiple_of(g * 8, 8), 8)
        for h in range(slots // CELL):
            lanes = slice(h * CELL, (h + 1) * CELL)
            cells = pl.ds(pl.multiple_of(h * remotes + g * 8, 8), 8)
            values = finished(acc_b, cells, [rpos[i, r, lanes] for i in range(3)])
            for i in range(4):
                back[i, r, lanes] = values[i]


def finished(acc, cells, pos):
    u = [sum(two_parts(x - 0.5)) for x in pos]
    total = acc[cells, 3, :]
    moments = [acc[cells, i, :] for i in range(3)]
    square = acc[cells, 4, :] + acc[cells, 5, :] + acc[cells, 6, :]
    norm = u[0] * u[0] + u[1] * u[1] + u[2] * u[2]
    dots = u[0] * moments[0] + u[1] * moments[1] + u[2] * moments[2]
    phi = (norm + SOFTEN) * total - 2.0 * dots + square
    return [phi] + [u[i] * total - moments[i] for i in range(3)]


def final_kernel(leaves, remotes, slots, acc, pos, q, occupied, send, back, out):
    @pl.loop(0, leaves // 8)
    def _(g):
        r = pl.ds(pl.multiple_of(g * 8, 8), 8)
        for h in range(slots // CELL):
            lanes = slice(h * CELL, (h + 1) * CELL)
            cells = pl.ds(pl.multiple_of(h * leaves + g * 8, 8), 8)
            values = finished(acc, cells, [pos[i, r, lanes] for i in range(3)])
            values[0] = values[0] - q[r, lanes] * (1.0 / np.sqrt(SOFTEN))
            for i in range(4):
                out[i, r, lanes] = values[i]

    if send is not None:
        def give(k, _):
            l = send[k]
            for i in range(4):
                out[i, pl.ds(l, 1), :] += back[i, pl.ds(k, 1), :]
            return 0
        lax.fori_loop(0, remotes, give, 0, unroll=8)

    @pl.loop(0, leaves // 8)
    def _(g):
        r = pl.ds(pl.multiple_of(g * 8, 8), 8)
        for i in range(4):
            out[i, r, :] = out[i, r, :] * occupied[r, :]


SMEM = pl.BlockSpec(memory_space=pltpu.SMEM)
VMEM = pl.BlockSpec(memory_space=pltpu.VMEM)
PARAMS = pltpu.CompilerParams(vmem_limit_bytes=58 << 20)


def scratch_loop(U):
    return [pltpu.VMEM((U, CELL, CELL), F32)] + [pltpu.VMEM((U, 2 * CELL, CELL), BF16)] * 2


def local_call(U, pos, q, counts, pairs, tables, npairs):
    leaves, slots = q.shape
    cells = 2 * leaves + 1
    return pl.pallas_call(
        functools.partial(local_kernel, U, leaves, slots, npairs),
        out_shape=(jax.ShapeDtypeStruct((cells, 8, CELL), F32), jax.ShapeDtypeStruct((cells, 32, CELL), BF16),
                   jax.ShapeDtypeStruct((cells, 16, CELL), BF16)),
        in_specs=[VMEM, VMEM, SMEM, SMEM, VMEM, VMEM, VMEM],
        out_specs=(VMEM, VMEM, VMEM),
        scratch_shapes=[pltpu.VMEM((cells, 16, CELL), BF16), pltpu.VMEM((2, 128, CELL), F32),
                        pltpu.VMEM((2, 128, CELL), F32), pltpu.VMEM((2, 256, CELL), F32),
                        pltpu.SMEM((2 * leaves + 9 * U,), jnp.int32),
                        pltpu.SMEM((leaves + 4 * npairs + 9 * U + 4,), jnp.int32)] + scratch_loop(U),
        compiler_params=PARAMS, name="local")(pos, q, counts, pairs, *tables)


def remote_call(U, rpos, counts, rcounts, pairs, tables, L, Q, acc, first, npairs):
    leaves = counts.shape[0]
    remotes, slots = rpos.shape[1:]
    cells = 2 * remotes + 1
    return pl.pallas_call(
        functools.partial(remote_kernel, U, leaves, remotes, slots, npairs, first),
        out_shape=(jax.ShapeDtypeStruct(acc.shape, F32), jax.ShapeDtypeStruct(rpos.shape, F32)),
        in_specs=[VMEM, SMEM, SMEM, SMEM, VMEM, VMEM, VMEM, VMEM, VMEM, VMEM],
        out_specs=(VMEM, VMEM),
        scratch_shapes=[pltpu.VMEM((cells, 16, CELL), BF16), pltpu.VMEM((cells, 16, CELL), BF16),
                        pltpu.VMEM((cells, 8, CELL), F32), pltpu.VMEM((2, 128, CELL), F32),
                        pltpu.VMEM((2, 128, CELL), F32),
                        pltpu.SMEM((4 * npairs + 9 * U + 4,), jnp.int32)] + scratch_loop(U),
        compiler_params=PARAMS, name="remote")(rpos, counts, rcounts, pairs, *tables, L, Q, acc)


def final_call(acc, pos, q, occupied, send, back):
    leaves, slots = q.shape
    remotes = back.shape[1]
    return pl.pallas_call(
        functools.partial(final_kernel, leaves, remotes, slots),
        out_shape=jax.ShapeDtypeStruct((4, leaves, slots), F32),
        in_specs=[VMEM, VMEM, VMEM, VMEM, SMEM, VMEM], out_specs=VMEM,
        compiler_params=PARAMS, name="final")(acc, pos, q, occupied, send, back)


def shifted(value, axis, by):
    length = lax.axis_size(axis)
    return lax.ppermute(value, axis, [(i, i + by) for i in range(length) if 0 <= i + by < length])


AXES = ("leaf", "grp")
GROUP = 16


def on_device(positions, charges, counts, send_left, pairs):
    leaves, slots = charges.shape
    remotes = send_left.shape[0]
    near = pairs.shape[1] - leaves - remotes
    occupied = (jnp.arange(slots)[None, :] < counts[:, None]).astype(jnp.float32)
    charges = charges * occupied
    tables = offset_tables()
    outgoing = jnp.take(jnp.concatenate([positions, charges[None]], 0), send_left, axis=1)
    remote = shifted(outgoing, AXES, -1)
    remote_counts = shifted(jnp.take(counts, send_left), AXES, -1)
    acc, L, Q = local_call(GROUP, positions, charges, counts, pairs, tables, near)
    acc, back = remote_call(GROUP, remote, counts, remote_counts, pairs, tables, L, Q, acc, leaves + near, remotes)
    returned = shifted(back, AXES, 1)
    return final_call(acc, positions, charges, occupied, send_left, returned)


def solution(mesh):
    in_specs = (P(None, AXES, None), P(AXES, None), P(AXES), P(AXES), P(None, AXES))
    return jax.shard_map(on_device, mesh=mesh, in_specs=in_specs, out_specs=P(None, AXES, None), check_vma=False)
```

```python
import functools
import numpy as np
import jax, jax.numpy as jnp
from jax import lax
from jax.experimental import pallas as pl
from jax.experimental.pallas import tpu as pltpu
from jax.sharding import PartitionSpec as P

F32 = jnp.float32
BF16 = jnp.bfloat16
SOFTEN = 0.05
CELL = 128
STEPS = 4
NN = (((1,), (0,)), ((), ()))
TN = (((0,), (0,)), ((), ()))


def offset_tables():
    code = np.arange(27)
    o = np.stack([code // 9 - 1, code // 3 % 3 - 1, code % 3 - 1], 1).astype(np.float32)
    scale = np.zeros((27, 16), np.float32)
    scale[:, 0:3] = 2 * o
    scale[:, 8:11] = 2 * o
    const = np.zeros((27, 16), np.float32)
    const[:, 3] = (o * o).sum(1)
    const[:, 4:7] = o
    const[:, 15] = 1
    const[:, 12:15] = o
    shift = np.zeros((27, 16), np.float32)
    shift[:, 0:3] = o
    shift[:, 4:7] = o * o
    shift[:, 12:15] = 2 * o
    wide = lambda t: np.broadcast_to(t[:, :, None], t.shape + (CELL,))
    return (jnp.asarray(wide(np.concatenate([scale, const], 1)), BF16),
            jnp.asarray(wide(np.concatenate([shift, shift[::-1]], 1)), F32))


def rounded(x):
    return x.astype(BF16).astype(F32)


def two_parts(x):
    high = rounded(x)
    return high, rounded(x - high)


def three_parts(x):
    high, middle = two_parts(x)
    return high, middle, x - high - middle


def features(pos, q, rows):
    highs, mids, coords = [], [], []
    for x in pos:
        high, mid = two_parts(x - 0.5)
        highs.append(high)
        mids.append(mid)
        coords.append(high + mid)
    squares = [c * c for c in coords]
    norm = squares[0] + squares[1] + squares[2]

    def put(part, row, value):
        rows[part, pl.ds(row, 8, stride=8), :] = value

    s = three_parts(norm)
    for i in range(3):
        for base in (0, 4):
            put(0, base + i, highs[i])
            put(1, base + i, mids[i])
    put(0, 3, jnp.ones_like(q))
    put(0, 7, s[0])
    put(1, 3, s[2])
    put(1, 7, s[1])
    for i in range(3):
        for row, value in ((i, coords[i]), (4 + i, squares[i])):
            high, mid = two_parts(q * value)
            put(2, row, high)
            put(3, row, mid)
    high, mid = two_parts(q)
    put(2, 3, high)
    put(3, 3, mid)
    put(2, 7, jnp.zeros_like(q))
    put(3, 7, jnp.zeros_like(q))
    if rows.shape[0] > 4:
        n = two_parts(norm + SOFTEN)
        for i in range(3):
            put(4, i, -2.0 * highs[i])
            put(4, 4 + i, -2.0 * mids[i])
        put(4, 3, n[0])
        put(4, 7, n[1])


def prepare(pos_at, q_at, leaves, slots, stage, R, Q, L):
    row = lax.broadcasted_iota(jnp.int32, (8, CELL), 0)
    coordinate = (row & 3) < 3

    @pl.loop(0, lax.div(leaves, 8))
    def _(g):
        first = pl.multiple_of(g * 8, 8)
        for h in range(slots // CELL):
            lanes = slice(h * CELL, (h + 1) * CELL)
            pos = [pos_at(i, pl.ds(first, 8), lanes) for i in range(3)]
            q = q_at(pl.ds(first, 8), lanes)
            features(pos, q, stage.at[h])
            for k in range(8):
                to = h * leaves + first + k
                at = slice(8 * k, 8 * k + 8)
                R[to] = jnp.concatenate([stage[h, 0, at, :], stage[h, 1, at, :]], 0).astype(BF16)
                Q[to] = jnp.concatenate([stage[h, 2, at, :], stage[h, 3, at, :]], 0).astype(BF16)
                if L is not None:
                    x = stage[h, 4, at, :]
                    first_half = jnp.where(row == 7, 1.0, x)
                    second = jnp.where(coordinate, x, 1.0)
                    third = jnp.where((row > 3) & (row < 7), pltpu.roll(x, 4, 0), 1.0)
                    fourth = jnp.where(row > 3, x, 1.0)
                    L[to] = jnp.concatenate([first_half, second, third, fourth], 0).astype(BF16)


def finish_list(lists, n, U, values):
    @pl.loop(0, (5 + STEPS) * U)
    def _(i):
        for r, v in zip(lists, values):
            r[n + i] = v


def pipeline(U, batches, aim, gram_operands, aimed, gram, weights, turned, last, middle):
    def step(j):
        if last is not None:
            for k in range(U):
                last(j * U + k, turned[k])
        for k in range(U):
            w = weights[k]
            middle((j + 1) * U + k, w)
            if last is not None:
                turned[k, 0:CELL] = w[0:CELL].T
                turned[k, CELL:] = w[CELL:].T
        for k in range(U):
            w = lax.rsqrt(gram[k])
            w3 = w * w * w
            high = w3.astype(BF16)
            weights[k, 0:CELL] = high
            weights[k, CELL:] = (w3 - high.astype(F32)).astype(BF16)
        for k in range(U):
            gram[k] = lax.dot_general(aimed[k], gram_operands((j + 3) * U + k), NN, preferred_element_type=F32)
        for k in range(U):
            aimed[k] = aim((j + 4) * U + k).T

    @pl.loop(0, lax.div(batches + 3 + STEPS, STEPS))
    def _(i):
        for s in range(STEPS):
            step(i * STEPS + s)


def summed(q, w):
    out = lax.dot_general(jnp.concatenate([q, q], 1), w, NN, preferred_element_type=F32)
    return out[0:8] + out[8:16]


def moved(m, shift, code, base):
    total = jnp.broadcast_to(m[3:4], m.shape)
    return m + shift[code, base : base + 8] * total + shift[code, base + 8 : base + 16] * pltpu.roll(m, 4, 0)


def cross_cells(U, lists, n, table, shift, L, Qa, acc_a, R, Qb, acc_b, scratch):
    la, lb, lc = lists

    def operands(i):
        b, c = lb[i], lc[i]
        r0 = R[b]
        return jnp.concatenate([r0, r0 * table[c, 0:16] + table[c, 16:32]], 0)

    def on_source(i, w):
        acc_b[lb[i]] += moved(summed(Qa[la[i]], w), shift, lc[i], 16)

    def on_target(i, w):
        acc_a[la[i]] += moved(summed(Qb[lb[i]], w), shift, lc[i], 0)

    pipeline(U, lax.div(n - 4 * U + U - 1, U), lambda i: L[la[i]], operands, *scratch, on_target, on_source)


def own_cells(U, cells, n, table, L, R, Q, acc, scratch):
    def operands(i):
        return jnp.concatenate([R[cells[i]], table[13, 16:32]], 0)

    def on_target(i, w):
        acc[cells[i]] += summed(Q[cells[i]], w)

    pipeline(U, lax.div(n - 4 * U + U - 1, U), lambda i: L[cells[i]], operands, *scratch, None, on_target)


def clear(aimed, gram, weights, turned):
    aimed[...] = jnp.zeros_like(aimed)
    gram[...] = jnp.ones_like(gram)
    weights[...] = jnp.zeros_like(weights)
    turned[...] = jnp.zeros_like(turned)


def start_list(lists, U, values):
    for r, v in zip(lists, values):
        for k in range(4 * U):
            r[k] = v


def list_pairs(lists, n, pairs, first, count, second_base, counts_a, counts_b, half_a, half_b):
    la, lb, lc = lists

    def body(i, n):
        a, b, code = pairs[0, i], pairs[1, i] - second_base, pairs[2, i]
        more_a = (counts_a[a] > CELL).astype(jnp.int32)
        more_b = (counts_b[b] > CELL).astype(jnp.int32)
        for da, db, more in ((0, 0, 1), (half_a, 0, more_a), (0, half_b, more_b), (half_a, half_b, more_a * more_b)):
            la[n] = a + da
            lb[n] = b + db
            lc[n] = code
            n = n + more
        return n

    return lax.fori_loop(first, first + count, body, n, unroll=4)


def idle_cell(L, R, Q, at_l, at_r):
    if L is not None:
        L[at_l] = jnp.ones(L.shape[1:], BF16)
    R[at_r] = jnp.zeros(R.shape[1:], BF16)
    Q[at_r] = jnp.zeros(Q.shape[1:], BF16)


def local_kernel(U, leaves, slots, npairs, pos, q, counts, pairs, table, shift, acc, L, Q, R, stage, own, la, lb, lc, *scratch):
    dummy = 2 * leaves
    lists = (la, lb, lc)
    acc[...] = jnp.zeros_like(acc)
    idle_cell(L, R, Q, dummy, dummy)
    clear(*scratch)
    start_list((own,), U, (dummy,))
    start_list(lists, U, (dummy, dummy, 13))
    prepare(lambda i, r, s: pos[i, r, s], lambda r, s: q[r, s], leaves, slots, stage, R, Q, L)

    def body(l, carry):
        n, nx = carry
        more = (counts[l] > CELL).astype(jnp.int32)
        own[n] = l
        own[n + 1] = l + leaves
        la[nx] = l
        lb[nx] = l + leaves
        lc[nx] = 13
        return n + 1 + more, nx + more

    n, nx = lax.fori_loop(0, leaves, body, (4 * U, 4 * U), unroll=8)
    nx = list_pairs(lists, nx, pairs, leaves, npairs, 0, counts, counts, leaves, leaves)
    finish_list((own,), n, U, (dummy,))
    finish_list(lists, nx, U, (dummy, dummy, 13))
    own_cells(U, own, n, table, L, R, Q, acc, scratch)
    clear(*scratch)
    cross_cells(U, lists, nx, table, shift, L, Q, acc, R, Q, acc, scratch)


def remote_kernel(U, leaves, remotes, slots, npairs, first, rpos, counts, rcounts, pairs, table, shift, L, Qa, acc_in,
                  acc, back, R, Q, acc_b, stage, la, lb, lc, *scratch):
    dummy_a, dummy_b = 2 * leaves, 2 * remotes
    lists = (la, lb, lc)
    acc[...] = acc_in[...]
    acc_b[...] = jnp.zeros_like(acc_b)
    idle_cell(None, R, Q, dummy_a, dummy_b)
    clear(*scratch)
    start_list(lists, U, (dummy_a, dummy_b, 13))
    prepare(lambda i, r, s: rpos[i, r, s], lambda r, s: rpos[3, r, s], remotes, slots, stage, R, Q, None)
    nx = list_pairs(lists, 4 * U, pairs, first, npairs, leaves, counts, rcounts, leaves, remotes)
    finish_list(lists, nx, U, (dummy_a, dummy_b, 13))
    cross_cells(U, lists, nx, table, shift, L, Qa, acc, R, Q, acc_b, scratch)

    @pl.loop(0, remotes // 8)
    def _(g):
        r = pl.ds(pl.multiple_of(g * 8, 8), 8)
        for h in range(slots // CELL):
            lanes = slice(h * CELL, (h + 1) * CELL)
            cells = pl.ds(pl.multiple_of(h * remotes + g * 8, 8), 8)
            values = finished(acc_b, cells, [rpos[i, r, lanes] for i in range(3)])
            for i in range(4):
                back[i, r, lanes] = values[i]


def finished(acc, cells, pos):
    u = [sum(two_parts(x - 0.5)) for x in pos]
    total = acc[cells, 3, :]
    moments = [acc[cells, i, :] for i in range(3)]
    square = acc[cells, 4, :] + acc[cells, 5, :] + acc[cells, 6, :]
    norm = u[0] * u[0] + u[1] * u[1] + u[2] * u[2]
    dots = u[0] * moments[0] + u[1] * moments[1] + u[2] * moments[2]
    phi = (norm + SOFTEN) * total - 2.0 * dots + square
    return [phi] + [u[i] * total - moments[i] for i in range(3)]


def final_kernel(leaves, remotes, slots, acc, pos, q, occupied, send, back, out):
    @pl.loop(0, leaves // 8)
    def _(g):
        r = pl.ds(pl.multiple_of(g * 8, 8), 8)
        for h in range(slots // CELL):
            lanes = slice(h * CELL, (h + 1) * CELL)
            cells = pl.ds(pl.multiple_of(h * leaves + g * 8, 8), 8)
            values = finished(acc, cells, [pos[i, r, lanes] for i in range(3)])
            values[0] = values[0] - q[r, lanes] * (1.0 / np.sqrt(SOFTEN))
            for i in range(4):
                out[i, r, lanes] = values[i]

    if send is not None:
        def give(k, _):
            l = send[k]
            for i in range(4):
                out[i, pl.ds(l, 1), :] += back[i, pl.ds(k, 1), :]
            return 0
        lax.fori_loop(0, remotes, give, 0, unroll=8)

    @pl.loop(0, leaves // 8)
    def _(g):
        r = pl.ds(pl.multiple_of(g * 8, 8), 8)
        for i in range(4):
            out[i, r, :] = out[i, r, :] * occupied[r, :]


SMEM = pl.BlockSpec(memory_space=pltpu.SMEM)
VMEM = pl.BlockSpec(memory_space=pltpu.VMEM)
PARAMS = pltpu.CompilerParams(vmem_limit_bytes=58 << 20)


def scratch_loop(U):
    return [pltpu.VMEM((U, CELL, 32), BF16), pltpu.VMEM((U, CELL, CELL), F32)] + [pltpu.VMEM((U, 2 * CELL, CELL), BF16)] * 2


def local_call(U, pos, q, counts, pairs, tables, npairs):
    leaves, slots = q.shape
    cells = 2 * leaves + 1
    return pl.pallas_call(
        functools.partial(local_kernel, U, leaves, slots, npairs),
        out_shape=(jax.ShapeDtypeStruct((cells, 8, CELL), F32), jax.ShapeDtypeStruct((cells, 32, CELL), BF16),
                   jax.ShapeDtypeStruct((cells, 16, CELL), BF16)),
        in_specs=[VMEM, VMEM, SMEM, SMEM, VMEM, VMEM],
        out_specs=(VMEM, VMEM, VMEM),
        scratch_shapes=[pltpu.VMEM((cells, 16, CELL), BF16), pltpu.VMEM((2, 5, 64, CELL), F32),
                        pltpu.SMEM((2 * leaves + (10 + STEPS) * U,), jnp.int32)]
        + [pltpu.SMEM((leaves + 4 * npairs + (10 + STEPS) * U,), jnp.int32)] * 3 + scratch_loop(U),
        compiler_params=PARAMS, name="local")(pos, q, counts, pairs, *tables)


def remote_call(U, rpos, counts, rcounts, pairs, tables, L, Q, acc, first, npairs):
    leaves = counts.shape[0]
    remotes, slots = rpos.shape[1:]
    cells = 2 * remotes + 1
    return pl.pallas_call(
        functools.partial(remote_kernel, U, leaves, remotes, slots, npairs, first),
        out_shape=(jax.ShapeDtypeStruct(acc.shape, F32), jax.ShapeDtypeStruct(rpos.shape, F32)),
        in_specs=[VMEM, SMEM, SMEM, SMEM, VMEM, VMEM, VMEM, VMEM, VMEM],
        out_specs=(VMEM, VMEM),
        scratch_shapes=[pltpu.VMEM((cells, 16, CELL), BF16), pltpu.VMEM((cells, 16, CELL), BF16),
                        pltpu.VMEM((cells, 8, CELL), F32), pltpu.VMEM((2, 4, 64, CELL), F32)]
        + [pltpu.SMEM((4 * npairs + (10 + STEPS) * U,), jnp.int32)] * 3 + scratch_loop(U),
        compiler_params=PARAMS, name="remote")(rpos, counts, rcounts, pairs, *tables, L, Q, acc)


def final_call(acc, pos, q, occupied, send, back):
    leaves, slots = q.shape
    remotes = back.shape[1]
    return pl.pallas_call(
        functools.partial(final_kernel, leaves, remotes, slots),
        out_shape=jax.ShapeDtypeStruct((4, leaves, slots), F32),
        in_specs=[VMEM, VMEM, VMEM, VMEM, SMEM, VMEM], out_specs=VMEM,
        compiler_params=PARAMS, name="final")(acc, pos, q, occupied, send, back)


def shifted(value, axis, by):
    length = lax.axis_size(axis)
    return lax.ppermute(value, axis, [(i, i + by) for i in range(length) if 0 <= i + by < length])


AXES = ("leaf", "grp")
GROUP = 8


def on_device(positions, charges, counts, send_left, pairs):
    leaves, slots = charges.shape
    remotes = send_left.shape[0]
    near = pairs.shape[1] - leaves - remotes
    occupied = (jnp.arange(slots)[None, :] < counts[:, None]).astype(jnp.float32)
    charges = charges * occupied
    tables = offset_tables()
    outgoing = jnp.take(jnp.concatenate([positions, charges[None]], 0), send_left, axis=1)
    remote = shifted(outgoing, AXES, -1)
    remote_counts = shifted(jnp.take(counts, send_left), AXES, -1)
    acc, L, Q = local_call(GROUP, positions, charges, counts, pairs, tables, near)
    acc, back = remote_call(GROUP, remote, counts, remote_counts, pairs, tables, L, Q, acc, leaves + near, remotes)
    returned = shifted(back, AXES, 1)
    return final_call(acc, positions, charges, occupied, send_left, returned)


def solution(mesh):
    in_specs = (P(None, AXES, None), P(AXES, None), P(AXES), P(AXES), P(None, AXES))
    return jax.shard_map(on_device, mesh=mesh, in_specs=in_specs, out_specs=P(None, AXES, None), check_vma=False)
```

```python
import functools
import numpy as np
import jax, jax.numpy as jnp
from jax import lax
from jax.experimental import pallas as pl
from jax.experimental.pallas import tpu as pltpu
from jax.sharding import PartitionSpec as P

F32 = jnp.float32
BF16 = jnp.bfloat16
SOFTEN = 0.05
CELL = 128
STEPS = 4
NN = (((1,), (0,)), ((), ()))
TN = (((0,), (0,)), ((), ()))


def offset_tables():
    code = np.arange(27)
    o = np.stack([code // 9 - 1, code // 3 % 3 - 1, code % 3 - 1], 1).astype(np.float32)
    scale = np.zeros((27, 16), np.float32)
    scale[:, 0:3] = 2 * o
    scale[:, 8:11] = 2 * o
    const = np.zeros((27, 16), np.float32)
    const[:, 3] = (o * o).sum(1)
    const[:, 4:7] = o
    const[:, 15] = 1
    const[:, 12:15] = o
    shift = np.zeros((27, 16), np.float32)
    shift[:, 0:3] = o
    shift[:, 4:7] = o * o
    shift[:, 12:15] = 2 * o
    wide = lambda t: np.broadcast_to(t[:, :, None], t.shape + (CELL,))
    return (jnp.asarray(wide(np.concatenate([scale, const], 1)), BF16),
            jnp.asarray(wide(np.concatenate([shift, shift[::-1]], 1)), F32))


def rounded(x):
    return x.astype(BF16).astype(F32)


def two_parts(x):
    high = rounded(x)
    return high, rounded(x - high)


def three_parts(x):
    high, middle = two_parts(x)
    return high, middle, x - high - middle


def features(pos, q, rows):
    highs, mids, coords = [], [], []
    for x in pos:
        high, mid = two_parts(x - 0.5)
        highs.append(high)
        mids.append(mid)
        coords.append(high + mid)
    squares = [c * c for c in coords]
    norm = squares[0] + squares[1] + squares[2]

    def put(part, row, value):
        rows[part, pl.ds(row, 8, stride=8), :] = value

    s = three_parts(norm)
    for i in range(3):
        for base in (0, 4):
            put(0, base + i, highs[i])
            put(1, base + i, mids[i])
    put(0, 3, jnp.ones_like(q))
    put(0, 7, s[0])
    put(1, 3, s[2])
    put(1, 7, s[1])
    for i in range(3):
        for row, value in ((i, coords[i]), (4 + i, squares[i])):
            high, mid = two_parts(q * value)
            put(2, row, high)
            put(3, row, mid)
    high, mid = two_parts(q)
    put(2, 3, high)
    put(3, 3, mid)
    put(2, 7, jnp.zeros_like(q))
    put(3, 7, jnp.zeros_like(q))
    if rows.shape[0] > 4:
        n = two_parts(norm + SOFTEN)
        for i in range(3):
            put(4, i, -2.0 * highs[i])
            put(4, 4 + i, -2.0 * mids[i])
        put(4, 3, n[0])
        put(4, 7, n[1])


def prepare(pos_at, q_at, leaves, slots, stage, R, Q, L, extra, carry):
    row = lax.broadcasted_iota(jnp.int32, (8, CELL), 0)
    coordinate = (row & 3) < 3

    def body(g, carry):
        carry = extra(g, carry)
        first = pl.multiple_of(g * 8, 8)
        for h in range(slots // CELL):
            lanes = slice(h * CELL, (h + 1) * CELL)
            pos = [pos_at(i, pl.ds(first, 8), lanes) for i in range(3)]
            q = q_at(pl.ds(first, 8), lanes)
            features(pos, q, stage.at[h])
            for k in range(8):
                to = h * leaves + first + k
                at = slice(8 * k, 8 * k + 8)
                R[to] = jnp.concatenate([stage[h, 0, at, :], stage[h, 1, at, :]], 0).astype(BF16)
                Q[to] = jnp.concatenate([stage[h, 2, at, :], stage[h, 3, at, :]], 0).astype(BF16)
                if L is not None:
                    x = stage[h, 4, at, :]
                    first_half = jnp.where(row == 7, 1.0, x)
                    second = jnp.where(coordinate, x, 1.0)
                    third = jnp.where((row > 3) & (row < 7), pltpu.roll(x, 4, 0), 1.0)
                    fourth = jnp.where(row > 3, x, 1.0)
                    L[to] = jnp.concatenate([first_half, second, third, fourth], 0).astype(BF16)
        return carry

    return lax.fori_loop(0, leaves // 8, body, carry)


def finish_list(lists, n, U, values):
    @pl.loop(0, (5 + STEPS) * U)
    def _(i):
        for r, v in zip(lists, values):
            r[n + i] = v


def pipeline(U, batches, aim, gram_operands, aimed, gram, weights, turned, last, middle):
    def step(j):
        if last is not None:
            for k in range(U):
                last(j * U + k, turned[k])
        for k in range(U):
            w = weights[k]
            middle((j + 1) * U + k, w)
            if last is not None:
                turned[k, 0:CELL] = w[0:CELL].T
                turned[k, CELL:] = w[CELL:].T
        for k in range(U):
            w = lax.rsqrt(gram[k])
            w3 = w * w * w
            high = w3.astype(BF16)
            weights[k, 0:CELL] = high
            weights[k, CELL:] = (w3 - high.astype(F32)).astype(BF16)
        for k in range(U):
            gram[k] = lax.dot_general(aimed[k], gram_operands((j + 3) * U + k), NN, preferred_element_type=F32)
        for k in range(U):
            aimed[k] = aim((j + 4) * U + k).T

    @pl.loop(0, lax.div(batches + 3 + STEPS, STEPS))
    def _(i):
        for s in range(STEPS):
            step(i * STEPS + s)


def summed(q, w):
    out = lax.dot_general(jnp.concatenate([q, q], 1), w, NN, preferred_element_type=F32)
    return out[0:8] + out[8:16]


def moved(m, shift, code, base):
    total = jnp.broadcast_to(m[3:4], m.shape)
    return m + shift[code, base : base + 8] * total + shift[code, base + 8 : base + 16] * pltpu.roll(m, 4, 0)


def cross_cells(U, lists, n, table, shift, L, Qa, acc_a, R, Qb, acc_b, scratch):
    la, lb, lc = lists

    def operands(i):
        b, c = lb[i], lc[i]
        r0 = R[b]
        return jnp.concatenate([r0, r0 * table[c, 0:16] + table[c, 16:32]], 0)

    def on_source(i, w):
        acc_b[lb[i]] += moved(summed(Qa[la[i]], w), shift, lc[i], 16)

    def on_target(i, w):
        acc_a[la[i]] += moved(summed(Qb[lb[i]], w), shift, lc[i], 0)

    pipeline(U, lax.div(n - 4 * U + U - 1, U), lambda i: L[la[i]], operands, *scratch, on_target, on_source)


def half_cells(U, leaves, cells, n, table, L, R, Q, acc, scratch):
    def second(i):
        return jnp.minimum(cells[i] + leaves, 2 * leaves)

    def operands(i):
        return jnp.concatenate([R[second(i)], table[13, 16:32]], 0)

    def on_source(i, w):
        acc[second(i)] += summed(Q[cells[i]], w)

    def on_target(i, w):
        acc[cells[i]] += summed(Q[second(i)], w)

    pipeline(U, lax.div(n - 4 * U + U - 1, U), lambda i: L[cells[i]], operands, *scratch, on_target, on_source)


def own_cells(U, cells, n, table, L, R, Q, acc, scratch):
    def operands(i):
        return jnp.concatenate([R[cells[i]], table[13, 16:32]], 0)

    def on_target(i, w):
        acc[cells[i]] += summed(Q[cells[i]], w)

    pipeline(U, lax.div(n - 4 * U + U - 1, U), lambda i: L[cells[i]], operands, *scratch, None, on_target)


def clear(aimed, gram, weights, turned):
    aimed[...] = jnp.zeros_like(aimed)
    gram[...] = jnp.ones_like(gram)
    weights[...] = jnp.zeros_like(weights)
    turned[...] = jnp.zeros_like(turned)


def start_list(lists, U, values):
    for r, v in zip(lists, values):
        for k in range(4 * U):
            r[k] = v


def list_pair(lists, n, pairs, i, second_base, counts_a, counts_b, half_a, half_b):
    la, lb, lc = lists
    a, b, code = pairs[0, i], pairs[1, i] - second_base, pairs[2, i]
    more_a = (counts_a[a] > CELL).astype(jnp.int32)
    more_b = (counts_b[b] > CELL).astype(jnp.int32)
    for da, db, more in ((0, 0, 1), (half_a, 0, more_a), (0, half_b, more_b), (half_a, half_b, more_a * more_b)):
        la[n] = a + da
        lb[n] = b + db
        lc[n] = code
        n = n + more
    return n


def idle_cell(L, R, Q, at_l, at_r):
    if L is not None:
        L[at_l] = jnp.ones(L.shape[1:], BF16)
    R[at_r] = jnp.zeros(R.shape[1:], BF16)
    Q[at_r] = jnp.zeros(Q.shape[1:], BF16)


def local_kernel(U, leaves, slots, npairs, pos, q, counts, pairs, table, shift, acc, L, Q, R, own, half, sizes, stage, la, lb,
                 lc, *scratch):
    dummy = 2 * leaves
    lists = (la, lb, lc)
    acc[...] = jnp.zeros_like(acc)
    idle_cell(L, R, Q, dummy, dummy)
    clear(*scratch)
    start_list((own, half), U, (dummy, dummy))
    start_list(lists, U, (dummy, dummy, 13))
    groups = leaves // 8
    share = npairs // groups

    def extra(g, carry):
        n, nh, nx = carry
        for k in range(8):
            l = 8 * g + k
            more = (counts[l] > CELL).astype(jnp.int32)
            own[n] = l
            own[n + 1] = l + leaves
            half[nh] = l
            n = n + 1 + more
            nh = nh + more
        for k in range(share):
            nx = list_pair(lists, nx, pairs, leaves + g * share + k, 0, counts, counts, leaves, leaves)
        return n, nh, nx

    n, nh, nx = prepare(lambda i, r, s: pos[i, r, s], lambda r, s: q[r, s], leaves, slots, stage, R, Q, L, extra,
                        (4 * U, 4 * U, 4 * U))
    nx = lax.fori_loop(leaves + groups * share, leaves + npairs, lambda i, nx: list_pair(
        lists, nx, pairs, i, 0, counts, counts, leaves, leaves), nx)
    finish_list((own,), n, U, (dummy,))
    finish_list((half,), nh, U, (dummy,))
    finish_list(lists, nx, U, (dummy, dummy, 13))
    sizes[0] = n
    sizes[1] = nh
    cross_cells(U, lists, nx, table, shift, L, Q, acc, R, Q, acc, scratch)


def own_kernel(U, leaves, own, half, sizes, table, L, R, Q, acc_in, acc, *scratch):
    clear(*scratch)
    half_cells(U, leaves, half, sizes[1], table, L, R, Q, acc, scratch)
    clear(*scratch)
    own_cells(U, own, sizes[0], table, L, R, Q, acc, scratch)


def remote_kernel(U, leaves, remotes, slots, npairs, first, rpos, counts, rcounts, pairs, table, shift, L, Qa, acc_in,
                  acc, back, R, Q, acc_b, stage, la, lb, lc, *scratch):
    dummy_a, dummy_b = 2 * leaves, 2 * remotes
    lists = (la, lb, lc)
    acc_b[...] = jnp.zeros_like(acc_b)
    idle_cell(None, R, Q, dummy_a, dummy_b)
    clear(*scratch)
    start_list(lists, U, (dummy_a, dummy_b, 13))
    groups = remotes // 8
    share = npairs // groups

    def extra(g, nx):
        for k in range(share):
            nx = list_pair(lists, nx, pairs, first + g * share + k, leaves, counts, rcounts, leaves, remotes)
        return nx

    nx = prepare(lambda i, r, s: rpos[i, r, s], lambda r, s: rpos[3, r, s], remotes, slots, stage, R, Q, None, extra, 4 * U)
    nx = lax.fori_loop(first + groups * share, first + npairs, lambda i, nx: list_pair(
        lists, nx, pairs, i, leaves, counts, rcounts, leaves, remotes), nx)
    finish_list(lists, nx, U, (dummy_a, dummy_b, 13))
    cross_cells(U, lists, nx, table, shift, L, Qa, acc, R, Q, acc_b, scratch)

    @pl.loop(0, remotes // 8)
    def _(g):
        r = pl.ds(pl.multiple_of(g * 8, 8), 8)
        for h in range(slots // CELL):
            lanes = slice(h * CELL, (h + 1) * CELL)
            cells = pl.ds(pl.multiple_of(h * remotes + g * 8, 8), 8)
            values = finished(acc_b, cells, [rpos[i, r, lanes] for i in range(3)])
            for i in range(4):
                back[i, r, lanes] = values[i]


def finished(acc, cells, pos):
    u = [sum(two_parts(x - 0.5)) for x in pos]
    total = acc[cells, 3, :]
    moments = [acc[cells, i, :] for i in range(3)]
    square = acc[cells, 4, :] + acc[cells, 5, :] + acc[cells, 6, :]
    norm = u[0] * u[0] + u[1] * u[1] + u[2] * u[2]
    dots = u[0] * moments[0] + u[1] * moments[1] + u[2] * moments[2]
    phi = (norm + SOFTEN) * total - 2.0 * dots + square
    return [phi] + [u[i] * total - moments[i] for i in range(3)]


def final_kernel(leaves, remotes, slots, acc, pos, q, occupied, send, back, out):
    @pl.loop(0, leaves // 8)
    def _(g):
        r = pl.ds(pl.multiple_of(g * 8, 8), 8)
        for h in range(slots // CELL):
            lanes = slice(h * CELL, (h + 1) * CELL)
            cells = pl.ds(pl.multiple_of(h * leaves + g * 8, 8), 8)
            values = finished(acc, cells, [pos[i, r, lanes] for i in range(3)])
            values[0] = values[0] - q[r, lanes] * (1.0 / np.sqrt(SOFTEN))
            for i in range(4):
                out[i, r, lanes] = values[i]

    if send is not None:
        def give(g, _):
            rows = [pl.ds(send[8 * g + k], 1) for k in range(8)]
            r = pl.ds(pl.multiple_of(g * 8, 8), 8)
            for i in range(4):
                extra = back[i, r, :]
                sums = [out[i, rows[k], :] + extra[k : k + 1] for k in range(8)]
                for k in range(8):
                    out[i, rows[k], :] = sums[k]
            return 0
        lax.fori_loop(0, remotes // 8, give, 0)

    @pl.loop(0, leaves // 8)
    def _(g):
        r = pl.ds(pl.multiple_of(g * 8, 8), 8)
        for i in range(4):
            out[i, r, :] = out[i, r, :] * occupied[r, :]


SMEM = pl.BlockSpec(memory_space=pltpu.SMEM)
VMEM = pl.BlockSpec(memory_space=pltpu.VMEM)
PARAMS = pltpu.CompilerParams(vmem_limit_bytes=20 << 20)


def scratch_loop(U):
    return [pltpu.VMEM((U, CELL, 32), BF16), pltpu.VMEM((U, CELL, CELL), F32)] + [pltpu.VMEM((U, 2 * CELL, CELL), BF16)] * 2


def pinned(x):
    return pltpu.with_memory_space_constraint(x, pltpu.VMEM)


def local_call(U, pos, q, counts, pairs, tables, npairs):
    leaves, slots = q.shape
    cells = 2 * leaves + 1
    room = (10 + STEPS) * U
    return pl.pallas_call(
        functools.partial(local_kernel, U, leaves, slots, npairs),
        out_shape=(pltpu.VMEM((cells, 8, CELL), F32), pltpu.VMEM((cells, 32, CELL), BF16),
                   pltpu.VMEM((cells, 16, CELL), BF16), pltpu.VMEM((cells, 16, CELL), BF16),
                   jax.ShapeDtypeStruct((2 * leaves + room,), jnp.int32), jax.ShapeDtypeStruct((leaves + room,), jnp.int32),
                   jax.ShapeDtypeStruct((2,), jnp.int32)),
        in_specs=[VMEM, VMEM, SMEM, SMEM, VMEM, VMEM],
        out_specs=(VMEM, VMEM, VMEM, VMEM, SMEM, SMEM, SMEM),
        scratch_shapes=[pltpu.VMEM((2, 5, 64, CELL), F32)]
        + [pltpu.SMEM((4 * npairs + room,), jnp.int32)] * 3 + scratch_loop(U),
        compiler_params=PARAMS, name="local")(pos, q, counts, pairs, *tables)


def remote_call(U, rpos, counts, rcounts, pairs, tables, L, Q, acc, first, npairs):
    leaves = counts.shape[0]
    remotes, slots = rpos.shape[1:]
    cells = 2 * remotes + 1
    return pl.pallas_call(
        functools.partial(remote_kernel, U, leaves, remotes, slots, npairs, first),
        out_shape=(pltpu.VMEM(acc.shape, F32), jax.ShapeDtypeStruct(rpos.shape, F32)),
        in_specs=[VMEM, SMEM, SMEM, SMEM, VMEM, VMEM, VMEM, VMEM, VMEM],
        out_specs=(VMEM, VMEM), input_output_aliases={8: 0},
        scratch_shapes=[pltpu.VMEM((cells, 16, CELL), BF16), pltpu.VMEM((cells, 16, CELL), BF16),
                        pltpu.VMEM((cells, 8, CELL), F32), pltpu.VMEM((2, 4, 64, CELL), F32)]
        + [pltpu.SMEM((4 * npairs + (10 + STEPS) * U,), jnp.int32)] * 3 + scratch_loop(U),
        compiler_params=PARAMS, name="remote")(rpos, counts, rcounts, pairs, *tables, pinned(L), pinned(Q), pinned(acc))


def own_call(U, own, half, sizes, tables, L, R, Q, acc):
    return pl.pallas_call(
        functools.partial(own_kernel, U, (acc.shape[0] - 1) // 2),
        out_shape=pltpu.VMEM(acc.shape, F32),
        in_specs=[SMEM, SMEM, SMEM, VMEM, VMEM, VMEM, VMEM, VMEM],
        out_specs=VMEM, input_output_aliases={7: 0}, scratch_shapes=scratch_loop(U),
        compiler_params=PARAMS, name="own")(own, half, sizes, tables[0], pinned(L), pinned(R), pinned(Q), pinned(acc))


def final_call(acc, pos, q, occupied, send, back):
    leaves, slots = q.shape
    remotes = back.shape[1]
    return pl.pallas_call(
        functools.partial(final_kernel, leaves, remotes, slots),
        out_shape=jax.ShapeDtypeStruct((4, leaves, slots), F32),
        in_specs=[VMEM, VMEM, VMEM, VMEM, SMEM, VMEM], out_specs=VMEM,
        compiler_params=PARAMS, name="final")(pinned(acc), pos, q, occupied, send, back)


def shifted(value, axis, by):
    length = lax.axis_size(axis)
    return lax.ppermute(value, axis, [(i, i + by) for i in range(length) if 0 <= i + by < length])


AXES = ("leaf", "grp")
GROUP = 8


def on_device(positions, charges, counts, send_left, pairs):
    leaves, slots = charges.shape
    remotes = send_left.shape[0]
    near = pairs.shape[1] - leaves - remotes
    occupied = (jnp.arange(slots)[None, :] < counts[:, None]).astype(jnp.float32)
    charges = charges * occupied
    tables = offset_tables()
    outgoing = jnp.take(jnp.concatenate([positions, charges[None]], 0), send_left, axis=1)
    remote = shifted(outgoing, AXES, -1)
    remote_counts = shifted(jnp.take(counts, send_left), AXES, -1)
    acc, L, Q, R, own, half, sizes = local_call(GROUP, positions, charges, counts, pairs, tables, near)
    acc, back = remote_call(GROUP, remote, counts, remote_counts, pairs, tables, L, Q, acc, leaves + near, remotes)
    returned = shifted(back, AXES, 1)
    acc = own_call(GROUP, own, half, sizes, tables, L, R, Q, acc)
    return final_call(acc, positions, charges, occupied, send_left, returned)


def solution(mesh):
    in_specs = (P(None, AXES, None), P(AXES, None), P(AXES), P(AXES), P(None, AXES))
    return jax.shard_map(on_device, mesh=mesh, in_specs=in_specs, out_specs=P(None, AXES, None), check_vma=False)
```

```python
import functools
import numpy as np
import jax, jax.numpy as jnp
from jax import lax
from jax.experimental import pallas as pl
from jax.experimental.pallas import tpu as pltpu
from jax.sharding import PartitionSpec as P

F32 = jnp.float32
BF16 = jnp.bfloat16
SOFTEN = 0.05
CELL = 128
STEPS = 4
UNROLL = 2
DIRECT = (7,)
NT = (((1,), (1,)), ((), ()))
NN = (((1,), (0,)), ((), ()))
TN = (((0,), (0,)), ((), ()))


def offset_tables():
    code = np.arange(27)
    o = np.stack([code // 9 - 1, code // 3 % 3 - 1, code % 3 - 1], 1).astype(np.float32)
    scale = np.zeros((27, 16), np.float32)
    scale[:, 0:3] = 2 * o
    scale[:, 8:11] = 2 * o
    const = np.zeros((27, 16), np.float32)
    const[:, 3] = (o * o).sum(1)
    const[:, 4:7] = o
    const[:, 15] = 1
    const[:, 12:15] = o
    shift = np.zeros((27, 16), np.float32)
    shift[:, 0:3] = o
    shift[:, 4:7] = o * o
    shift[:, 12:15] = 2 * o
    wide = lambda t: np.broadcast_to(t[:, :, None], t.shape + (CELL,))
    return (jnp.asarray(wide(np.concatenate([scale, const], 1)), BF16),
            jnp.asarray(wide(np.concatenate([shift, shift[::-1]], 1)), F32))


def rounded(x):
    return x.astype(BF16).astype(F32)


def two_parts(x):
    high = rounded(x)
    return high, rounded(x - high)


def three_parts(x):
    high, middle = two_parts(x)
    return high, middle, x - high - middle


def features(pos, q, rows):
    highs, mids, coords = [], [], []
    for x in pos:
        high, mid = two_parts(x - 0.5)
        highs.append(high)
        mids.append(mid)
        coords.append(high + mid)
    squares = [c * c for c in coords]
    norm = squares[0] + squares[1] + squares[2]

    def put(part, row, value):
        rows[part, pl.ds(row, 8, stride=8), :] = value

    s = three_parts(norm)
    for i in range(3):
        for base in (0, 4):
            put(0, base + i, highs[i])
            put(1, base + i, mids[i])
    put(0, 3, jnp.ones_like(q))
    put(0, 7, s[0])
    put(1, 3, s[2])
    put(1, 7, s[1])
    for i in range(3):
        for row, value in ((i, coords[i]), (4 + i, squares[i])):
            high, mid = two_parts(q * value)
            put(2, row, high)
            put(3, row, mid)
    high, mid = two_parts(q)
    put(2, 3, high)
    put(3, 3, mid)
    put(2, 7, jnp.zeros_like(q))
    put(3, 7, jnp.zeros_like(q))
    if rows.shape[0] > 4:
        n = two_parts(norm + SOFTEN)
        for i in range(3):
            put(4, i, -2.0 * highs[i])
            put(4, 4 + i, -2.0 * mids[i])
        put(4, 3, n[0])
        put(4, 7, n[1])


def prepare(pos_at, q_at, leaves, slots, stage, R, Q, L, extra, carry):
    row = lax.broadcasted_iota(jnp.int32, (8, CELL), 0)
    coordinate = (row & 3) < 3

    def body(g, carry):
        carry = extra(g, carry)
        first = pl.multiple_of(g * 8, 8)
        for h in range(slots // CELL):
            lanes = slice(h * CELL, (h + 1) * CELL)
            pos = [pos_at(i, pl.ds(first, 8), lanes) for i in range(3)]
            q = q_at(pl.ds(first, 8), lanes)
            features(pos, q, stage.at[h])
            for k in range(8):
                to = h * leaves + first + k
                at = slice(8 * k, 8 * k + 8)
                R[to] = jnp.concatenate([stage[h, 0, at, :], stage[h, 1, at, :]], 0).astype(BF16)
                Q[to] = jnp.concatenate([stage[h, 2, at, :], stage[h, 3, at, :]], 0).astype(BF16)
                if L is not None:
                    x = stage[h, 4, at, :]
                    first_half = jnp.where(row == 7, 1.0, x)
                    second = jnp.where(coordinate, x, 1.0)
                    third = jnp.where((row > 3) & (row < 7), pltpu.roll(x, 4, 0), 1.0)
                    fourth = jnp.where(row > 3, x, 1.0)
                    L[to] = jnp.concatenate([first_half, second, third, fourth], 0).astype(BF16)
        return carry

    return lax.fori_loop(0, leaves // 8, body, carry, unroll=UNROLL)


def finish_list(lists, n, U, values):
    @pl.loop(0, (5 + STEPS) * U)
    def _(i):
        for r, v in zip(lists, values):
            r[n + i] = v


def pipeline(U, batches, aim, gram_operands, aimed, gram, weights, turned, wide, last, middle):
    def step(j):
        if last is not None:
            for k in range(U):
                if k not in DIRECT:
                    last(j * U + k, turned[k], NN)
        for k in range(U):
            w = weights[k]
            middle((j + 1) * U + k, w)
            if last is not None and k in DIRECT:
                last((j + 1) * U + k, wide[k], NT)
            elif last is not None:
                turned[k, 0:CELL] = w[0:CELL].T
                turned[k, CELL:] = w[CELL:].T
        for k in range(U):
            w = lax.rsqrt(gram[k])
            w3 = w * w * w
            high = w3.astype(BF16)
            low = (w3 - high.astype(F32)).astype(BF16)
            weights[k, 0:CELL] = high
            weights[k, CELL:] = low
            if last is not None and k in DIRECT:
                wide[k, :, 0:CELL] = high
                wide[k, :, CELL:] = low
        for k in range(U):
            gram[k] = lax.dot_general(aimed[k], gram_operands((j + 3) * U + k), NN, preferred_element_type=F32)
        for k in range(U):
            aimed[k] = aim((j + 4) * U + k).T

    @pl.loop(0, lax.div(batches + 3 + STEPS, STEPS))
    def _(i):
        for s in range(STEPS):
            step(i * STEPS + s)


def summed(q, w, form=NN):
    out = lax.dot_general(jnp.concatenate([q, q], 1), w, form, preferred_element_type=F32)
    return out[0:8] + out[8:16]


def moved(m, shift, code, base):
    total = jnp.broadcast_to(m[3:4], m.shape)
    return m + shift[code, base : base + 8] * total + shift[code, base + 8 : base + 16] * pltpu.roll(m, 4, 0)


def cross_cells(U, lists, n, table, shift, L, Qa, acc_a, R, Qb, acc_b, scratch):
    la, lb, lc = lists

    def operands(i):
        b, c = lb[i], lc[i]
        r0 = R[b]
        return jnp.concatenate([r0, r0 * table[c, 0:16] + table[c, 16:32]], 0)

    def on_source(i, w):
        acc_b[lb[i]] += moved(summed(Qa[la[i]], w), shift, lc[i], 16)

    def on_target(i, w, form):
        acc_a[la[i]] += moved(summed(Qb[lb[i]], w, form), shift, lc[i], 0)

    pipeline(U, lax.div(n - 4 * U + U - 1, U), lambda i: L[la[i]], operands, *scratch, on_target, on_source)


def half_cells(U, leaves, cells, n, table, L, R, Q, acc, scratch):
    def second(i):
        return jnp.minimum(cells[i] + leaves, 2 * leaves)

    def operands(i):
        return jnp.concatenate([R[second(i)], table[13, 16:32]], 0)

    def on_source(i, w):
        acc[second(i)] += summed(Q[cells[i]], w)

    def on_target(i, w, form):
        acc[cells[i]] += summed(Q[second(i)], w, form)

    pipeline(U, lax.div(n - 4 * U + U - 1, U), lambda i: L[cells[i]], operands, *scratch, on_target, on_source)


def own_cells(U, cells, n, table, L, R, Q, acc, scratch):
    def operands(i):
        return jnp.concatenate([R[cells[i]], table[13, 16:32]], 0)

    def on_target(i, w):
        acc[cells[i]] += summed(Q[cells[i]], w)

    pipeline(U, lax.div(n - 4 * U + U - 1, U), lambda i: L[cells[i]], operands, *scratch, None, on_target)


def clear(aimed, gram, weights, turned, wide):
    aimed[...] = jnp.zeros_like(aimed)
    gram[...] = jnp.ones_like(gram)
    weights[...] = jnp.zeros_like(weights)
    turned[...] = jnp.zeros_like(turned)
    wide[...] = jnp.zeros_like(wide)


def start_list(lists, U, values):
    for r, v in zip(lists, values):
        for k in range(4 * U):
            r[k] = v


def list_pair(lists, n, pairs, i, second_base, counts_a, counts_b, half_a, half_b):
    la, lb, lc = lists
    a, b, code = pairs[0, i], pairs[1, i] - second_base, pairs[2, i]
    more_a = (counts_a[a] > CELL).astype(jnp.int32)
    more_b = (counts_b[b] > CELL).astype(jnp.int32)
    for da, db, more in ((0, 0, 1), (half_a, 0, more_a), (0, half_b, more_b), (half_a, half_b, more_a * more_b)):
        la[n] = a + da
        lb[n] = b + db
        lc[n] = code
        n = n + more
    return n


def idle_cell(L, R, Q, at_l, at_r):
    if L is not None:
        L[at_l] = jnp.ones(L.shape[1:], BF16)
    R[at_r] = jnp.zeros(R.shape[1:], BF16)
    Q[at_r] = jnp.zeros(Q.shape[1:], BF16)


def local_kernel(U, leaves, slots, npairs, pos, q, counts, pairs, table, shift, acc, L, Q, R, own, half, sizes, stage, la, lb,
                 lc, *scratch):
    dummy = 2 * leaves
    lists = (la, lb, lc)
    acc[...] = jnp.zeros_like(acc)
    idle_cell(L, R, Q, dummy, dummy)
    clear(*scratch)
    start_list((own, half), U, (dummy, dummy))
    start_list(lists, U, (dummy, dummy, 13))
    groups = leaves // 8
    share = npairs // groups

    def extra(g, carry):
        n, nh, nx = carry
        for k in range(8):
            l = 8 * g + k
            more = (counts[l] > CELL).astype(jnp.int32)
            own[n] = l
            own[n + 1] = l + leaves
            half[nh] = l
            n = n + 1 + more
            nh = nh + more
        for k in range(share):
            nx = list_pair(lists, nx, pairs, leaves + g * share + k, 0, counts, counts, leaves, leaves)
        return n, nh, nx

    n, nh, nx = prepare(lambda i, r, s: pos[i, r, s], lambda r, s: q[r, s], leaves, slots, stage, R, Q, L, extra,
                        (4 * U, 4 * U, 4 * U))
    nx = lax.fori_loop(leaves + groups * share, leaves + npairs, lambda i, nx: list_pair(
        lists, nx, pairs, i, 0, counts, counts, leaves, leaves), nx)
    finish_list((own,), n, U, (dummy,))
    finish_list((half,), nh, U, (dummy,))
    finish_list(lists, nx, U, (dummy, dummy, 13))
    sizes[0] = n
    sizes[1] = nh
    cross_cells(U, lists, nx, table, shift, L, Q, acc, R, Q, acc, scratch)


def own_kernel(U, leaves, own, half, sizes, table, L, R, Q, acc_in, acc, *scratch):
    clear(*scratch)
    half_cells(U, leaves, half, sizes[1], table, L, R, Q, acc, scratch)
    clear(*scratch)
    own_cells(U, own, sizes[0], table, L, R, Q, acc, scratch)


def remote_kernel(U, leaves, remotes, slots, npairs, first, rpos, counts, rcounts, pairs, table, shift, L, Qa, acc_in,
                  acc, back, R, Q, acc_b, stage, la, lb, lc, *scratch):
    dummy_a, dummy_b = 2 * leaves, 2 * remotes
    lists = (la, lb, lc)
    acc_b[...] = jnp.zeros_like(acc_b)
    idle_cell(None, R, Q, dummy_a, dummy_b)
    clear(*scratch)
    start_list(lists, U, (dummy_a, dummy_b, 13))
    groups = remotes // 8
    share = npairs // groups

    def extra(g, nx):
        for k in range(share):
            nx = list_pair(lists, nx, pairs, first + g * share + k, leaves, counts, rcounts, leaves, remotes)
        return nx

    nx = prepare(lambda i, r, s: rpos[i, r, s], lambda r, s: rpos[3, r, s], remotes, slots, stage, R, Q, None, extra, 4 * U)
    nx = lax.fori_loop(first + groups * share, first + npairs, lambda i, nx: list_pair(
        lists, nx, pairs, i, leaves, counts, rcounts, leaves, remotes), nx)
    finish_list(lists, nx, U, (dummy_a, dummy_b, 13))
    cross_cells(U, lists, nx, table, shift, L, Qa, acc, R, Q, acc_b, scratch)

    @pl.loop(0, remotes // 8)
    def _(g):
        r = pl.ds(pl.multiple_of(g * 8, 8), 8)
        for h in range(slots // CELL):
            lanes = slice(h * CELL, (h + 1) * CELL)
            cells = pl.ds(pl.multiple_of(h * remotes + g * 8, 8), 8)
            values = finished(acc_b, cells, [rpos[i, r, lanes] for i in range(3)])
            for i in range(4):
                back[i, r, lanes] = values[i]


def finished(acc, cells, pos):
    u = [sum(two_parts(x - 0.5)) for x in pos]
    total = acc[cells, 3, :]
    moments = [acc[cells, i, :] for i in range(3)]
    square = acc[cells, 4, :] + acc[cells, 5, :] + acc[cells, 6, :]
    norm = u[0] * u[0] + u[1] * u[1] + u[2] * u[2]
    dots = u[0] * moments[0] + u[1] * moments[1] + u[2] * moments[2]
    phi = (norm + SOFTEN) * total - 2.0 * dots + square
    return [phi] + [u[i] * total - moments[i] for i in range(3)]


def final_kernel(leaves, remotes, slots, acc, pos, q, occupied, send, back, out):
    @pl.loop(0, leaves // 8)
    def _(g):
        r = pl.ds(pl.multiple_of(g * 8, 8), 8)
        for h in range(slots // CELL):
            lanes = slice(h * CELL, (h + 1) * CELL)
            cells = pl.ds(pl.multiple_of(h * leaves + g * 8, 8), 8)
            values = finished(acc, cells, [pos[i, r, lanes] for i in range(3)])
            values[0] = values[0] - q[r, lanes] * (1.0 / np.sqrt(SOFTEN))
            for i in range(4):
                out[i, r, lanes] = values[i]

    if send is not None:
        def give(g, _):
            rows = [pl.ds(send[8 * g + k], 1) for k in range(8)]
            r = pl.ds(pl.multiple_of(g * 8, 8), 8)
            for i in range(4):
                extra = back[i, r, :]
                sums = [out[i, rows[k], :] + extra[k : k + 1] for k in range(8)]
                for k in range(8):
                    out[i, rows[k], :] = sums[k]
            return 0
        lax.fori_loop(0, remotes // 8, give, 0)

    @pl.loop(0, leaves // 8)
    def _(g):
        r = pl.ds(pl.multiple_of(g * 8, 8), 8)
        for i in range(4):
            out[i, r, :] = out[i, r, :] * occupied[r, :]


SMEM = pl.BlockSpec(memory_space=pltpu.SMEM)
VMEM = pl.BlockSpec(memory_space=pltpu.VMEM)
PARAMS = pltpu.CompilerParams(vmem_limit_bytes=20 << 20)


def scratch_loop(U):
    return [pltpu.VMEM((U, CELL, 32), BF16), pltpu.VMEM((U, CELL, CELL), F32)] + [pltpu.VMEM((U, 2 * CELL, CELL), BF16)] * 2 + [pltpu.VMEM((U, CELL, 2 * CELL), BF16)]


def gather_kernel(remotes, pos, q, counts, send, out):
    lane = lax.broadcasted_iota(jnp.int32, (1, q.shape[1]), 1)

    def body(g, _):
        for k in range(8):
            to, at = pl.ds(8 * g + k, 1), send[8 * g + k]
            row, here = pl.ds(at, 1), lane < counts[at]
            out[0, to, :] = jnp.where(here, pos[0, row, :], 2.0)
            out[1, to, :] = pos[1, row, :]
            out[2, to, :] = pos[2, row, :]
            out[3, to, :] = jnp.where(here, q[row, :], 0.0)
        return 0

    lax.fori_loop(0, remotes // 8, body, 0)


def gather_call(pos, q, counts, send):
    return pl.pallas_call(
        functools.partial(gather_kernel, send.shape[0]),
        out_shape=jax.ShapeDtypeStruct((4, send.shape[0], q.shape[1]), F32),
        in_specs=[VMEM, VMEM, SMEM, SMEM], out_specs=VMEM, compiler_params=PARAMS, name="gather")(pos, q, counts, send)


def pinned(x):
    return pltpu.with_memory_space_constraint(x, pltpu.VMEM)


def local_call(U, pos, q, counts, pairs, tables, npairs):
    leaves, slots = q.shape
    cells = 2 * leaves + 1
    room = (10 + STEPS) * U
    return pl.pallas_call(
        functools.partial(local_kernel, U, leaves, slots, npairs),
        out_shape=(pltpu.VMEM((cells, 8, CELL), F32), pltpu.VMEM((cells, 32, CELL), BF16),
                   pltpu.VMEM((cells, 16, CELL), BF16), pltpu.VMEM((cells, 16, CELL), BF16),
                   jax.ShapeDtypeStruct((2 * leaves + room,), jnp.int32), jax.ShapeDtypeStruct((leaves + room,), jnp.int32),
                   jax.ShapeDtypeStruct((2,), jnp.int32)),
        in_specs=[VMEM, VMEM, SMEM, SMEM, VMEM, VMEM],
        out_specs=(VMEM, VMEM, VMEM, VMEM, SMEM, SMEM, SMEM),
        scratch_shapes=[pltpu.VMEM((2, 5, 64, CELL), F32)]
        + [pltpu.SMEM((4 * npairs + room,), jnp.int32)] * 3 + scratch_loop(U),
        compiler_params=PARAMS, name="local")(pos, q, counts, pairs, *tables)


def remote_call(U, rpos, counts, rcounts, pairs, tables, L, Q, acc, first, npairs):
    leaves = counts.shape[0]
    remotes, slots = rpos.shape[1:]
    cells = 2 * remotes + 1
    return pl.pallas_call(
        functools.partial(remote_kernel, U, leaves, remotes, slots, npairs, first),
        out_shape=(pltpu.VMEM(acc.shape, F32), jax.ShapeDtypeStruct(rpos.shape, F32)),
        in_specs=[VMEM, SMEM, SMEM, SMEM, VMEM, VMEM, VMEM, VMEM, VMEM],
        out_specs=(VMEM, VMEM), input_output_aliases={8: 0},
        scratch_shapes=[pltpu.VMEM((cells, 16, CELL), BF16), pltpu.VMEM((cells, 16, CELL), BF16),
                        pltpu.VMEM((cells, 8, CELL), F32), pltpu.VMEM((2, 4, 64, CELL), F32)]
        + [pltpu.SMEM((4 * npairs + (10 + STEPS) * U,), jnp.int32)] * 3 + scratch_loop(U),
        compiler_params=PARAMS, name="remote")(rpos, counts, rcounts, pairs, *tables, pinned(L), pinned(Q), pinned(acc))


def own_call(U, own, half, sizes, tables, L, R, Q, acc):
    return pl.pallas_call(
        functools.partial(own_kernel, U, (acc.shape[0] - 1) // 2),
        out_shape=pltpu.VMEM(acc.shape, F32),
        in_specs=[SMEM, SMEM, SMEM, VMEM, VMEM, VMEM, VMEM, VMEM],
        out_specs=VMEM, input_output_aliases={7: 0}, scratch_shapes=scratch_loop(U),
        compiler_params=PARAMS, name="own")(own, half, sizes, tables[0], pinned(L), pinned(R), pinned(Q), pinned(acc))


def final_call(acc, pos, q, occupied, send, back):
    leaves, slots = q.shape
    remotes = back.shape[1]
    return pl.pallas_call(
        functools.partial(final_kernel, leaves, remotes, slots),
        out_shape=jax.ShapeDtypeStruct((4, leaves, slots), F32),
        in_specs=[VMEM, VMEM, VMEM, VMEM, SMEM, VMEM], out_specs=VMEM,
        compiler_params=PARAMS, name="final")(pinned(acc), pos, q, occupied, send, back)


def shifted(value, axis, by):
    length = lax.axis_size(axis)
    return lax.ppermute(value, axis, [(i, i + by) for i in range(length) if 0 <= i + by < length])


AXES = ("leaf", "grp")
GROUP = 8


def on_device(positions, charges, counts, send_left, pairs):
    leaves, slots = charges.shape
    remotes = send_left.shape[0]
    near = pairs.shape[1] - leaves - remotes
    remote = shifted(gather_call(positions, charges, counts, send_left), AXES, -1)
    occupied = (jnp.arange(slots)[None, :] < counts[:, None]).astype(jnp.float32)
    charges = charges * occupied
    tables = offset_tables()
    empty = (remote[0, :, CELL] > 1.5) | (lax.axis_index(AXES) == lax.axis_size(AXES) - 1)
    remote_counts = jnp.where(empty, 0, slots).astype(jnp.int32)
    acc, L, Q, R, own, half, sizes = local_call(GROUP, positions, charges, counts, pairs, tables, near)
    acc, back = remote_call(GROUP, remote, counts, remote_counts, pairs, tables, L, Q, acc, leaves + near, remotes)
    returned = shifted(back, AXES, 1)
    acc = own_call(GROUP, own, half, sizes, tables, L, R, Q, acc)
    return final_call(acc, positions, charges, occupied, send_left, returned)


def solution(mesh):
    in_specs = (P(None, AXES, None), P(AXES, None), P(AXES), P(AXES), P(None, AXES))
    return jax.shard_map(on_device, mesh=mesh, in_specs=in_specs, out_specs=P(None, AXES, None), check_vma=False)
```

```python
import functools
import numpy as np
import jax, jax.numpy as jnp
from jax import lax
from jax.experimental import pallas as pl
from jax.experimental.pallas import tpu as pltpu
from jax.sharding import PartitionSpec as P

F32 = jnp.float32
BF16 = jnp.bfloat16
SOFTEN = 0.05
CELL = 128
UNROLL = 2
NT = (((1,), (1,)), ((), ()))
NN = (((1,), (0,)), ((), ()))
TN = (((0,), (0,)), ((), ()))


def offset_tables():
    code = np.arange(27)
    o = np.stack([code // 9 - 1, code // 3 % 3 - 1, code % 3 - 1], 1).astype(np.float32)
    scale = np.zeros((27, 16), np.float32)
    scale[:, 0:3] = 2 * o
    scale[:, 8:11] = 2 * o
    const = np.zeros((27, 16), np.float32)
    const[:, 3] = (o * o).sum(1)
    const[:, 4:7] = o
    const[:, 15] = 1
    const[:, 12:15] = o
    shift = np.zeros((27, 16), np.float32)
    shift[:, 0:3] = o
    shift[:, 4:7] = o * o
    shift[:, 12:15] = 2 * o
    wide = lambda t: np.broadcast_to(t[:, :, None], t.shape + (CELL,))
    return (jnp.asarray(wide(np.concatenate([scale, const], 1)), BF16),
            jnp.asarray(wide(np.concatenate([shift, shift[::-1]], 1)), F32))


def rounded(x):
    return x.astype(BF16).astype(F32)


def two_parts(x):
    high = rounded(x)
    return high, rounded(x - high)


def three_parts(x):
    high, middle = two_parts(x)
    return high, middle, x - high - middle


def features(pos, q, rows):
    highs, mids, coords = [], [], []
    for x in pos:
        high, mid = two_parts(x - 0.5)
        highs.append(high)
        mids.append(mid)
        coords.append(high + mid)
    squares = [c * c for c in coords]
    norm = squares[0] + squares[1] + squares[2]

    def put(part, row, value):
        rows[part, pl.ds(row, 8, stride=8), :] = value

    s = three_parts(norm)
    for i in range(3):
        for base in (0, 4):
            put(0, base + i, highs[i])
            put(1, base + i, mids[i])
    put(0, 3, jnp.ones_like(q))
    put(0, 7, s[0])
    put(1, 3, s[2])
    put(1, 7, s[1])
    for i in range(3):
        for row, value in ((i, coords[i]), (4 + i, squares[i])):
            high, mid = two_parts(q * value)
            put(2, row, high)
            put(3, row, mid)
    high, mid = two_parts(q)
    put(2, 3, high)
    put(3, 3, mid)
    put(2, 7, jnp.zeros_like(q))
    put(3, 7, jnp.zeros_like(q))
    if rows.shape[0] > 4:
        n = two_parts(norm + SOFTEN)
        for i in range(3):
            put(4, i, -2.0 * highs[i])
            put(4, 4 + i, -2.0 * mids[i])
        put(4, 3, n[0])
        put(4, 7, n[1])


def prepare(pos_at, q_at, leaves, slots, stage, R, Q, L, extra, carry):
    row = lax.broadcasted_iota(jnp.int32, (8, CELL), 0)
    coordinate = (row & 3) < 3

    def body(g, carry):
        carry = extra(g, carry)
        first = pl.multiple_of(g * 8, 8)
        for h in range(slots // CELL):
            lanes = slice(h * CELL, (h + 1) * CELL)
            pos = [pos_at(i, pl.ds(first, 8), lanes) for i in range(3)]
            q = q_at(pl.ds(first, 8), lanes)
            features(pos, q, stage.at[h])
            for k in range(8):
                to = h * leaves + first + k
                at = slice(8 * k, 8 * k + 8)
                R[to] = jnp.concatenate([stage[h, 0, at, :], stage[h, 1, at, :]], 0).astype(BF16)
                Q[to] = jnp.concatenate([stage[h, 2, at, :], stage[h, 3, at, :]], 0).astype(BF16)
                if L is not None:
                    x = stage[h, 4, at, :]
                    first_half = jnp.where(row == 7, 1.0, x)
                    second = jnp.where(coordinate, x, 1.0)
                    third = jnp.where((row > 3) & (row < 7), pltpu.roll(x, 4, 0), 1.0)
                    fourth = jnp.where(row > 3, x, 1.0)
                    L[to] = jnp.concatenate([first_half, second, third, fourth], 0).astype(BF16)
        return carry

    return lax.fori_loop(0, leaves // 8, body, carry, unroll=UNROLL)


def finish_list(lists, n, U, values):
    @pl.loop(0, (5 + U) * U)
    def _(i):
        for r, v in zip(lists, values):
            r[n + i] = v


def pipeline(U, batches, aim, gram_operands, aimed, gram, weights, turned, wide, last, middle):
    def step(j):
        if last is not None:
            for k in range(U):
                if k < U - 1:
                    last(j * U + k, turned[k], NN)
        for k in range(U):
            w = weights[k]
            middle((j + 1) * U + k, w)
            if last is not None and k == U - 1:
                last((j + 1) * U + k, wide[k], NT)
            elif last is not None:
                turned[k, 0:CELL] = w[0:CELL].T
                turned[k, CELL:] = w[CELL:].T
        for k in range(U):
            w = lax.rsqrt(gram[k])
            w3 = w * w * w
            high = w3.astype(BF16)
            low = (w3 - high.astype(F32)).astype(BF16)
            weights[k, 0:CELL] = high
            weights[k, CELL:] = low
            if last is not None and k == U - 1:
                wide[k, :, 0:CELL] = high
                wide[k, :, CELL:] = low
        for k in range(U):
            gram[k] = lax.dot_general(aimed[k], gram_operands((j + 3) * U + k), NN, preferred_element_type=F32)
        for k in range(U):
            aimed[k] = aim((j + 4) * U + k).T

    @pl.loop(0, lax.div(batches + 3 + U, U))
    def _(i):
        for s in range(U):
            step(i * U + s)


def summed(q, w, form=NN):
    out = lax.dot_general(jnp.concatenate([q, q], 1), w, form, preferred_element_type=F32)
    return out[0:8] + out[8:16]


def moved(m, shift, code, base):
    total = jnp.broadcast_to(m[3:4], m.shape)
    return m + shift[code, base : base + 8] * total + shift[code, base + 8 : base + 16] * pltpu.roll(m, 4, 0)


def cross_cells(U, lists, n, table, shift, L, Qa, acc_a, R, Qb, acc_b, scratch):
    la, lb, lc = lists

    def operands(i):
        b, c = lb[i], lc[i]
        r0 = R[b]
        return jnp.concatenate([r0, r0 * table[c, 0:16] + table[c, 16:32]], 0)

    def on_source(i, w):
        acc_b[lb[i]] += moved(summed(Qa[la[i]], w), shift, lc[i], 16)

    def on_target(i, w, form):
        acc_a[la[i]] += moved(summed(Qb[lb[i]], w, form), shift, lc[i], 0)

    pipeline(U, lax.div(n - 4 * U + U - 1, U), lambda i: L[la[i]], operands, *scratch, on_target, on_source)


def half_cells(U, leaves, cells, n, table, L, R, Q, acc, scratch):
    def second(i):
        return jnp.minimum(cells[i] + leaves, 2 * leaves)

    def operands(i):
        return jnp.concatenate([R[second(i)], table[13, 16:32]], 0)

    def on_source(i, w):
        acc[second(i)] += summed(Q[cells[i]], w)

    def on_target(i, w, form):
        acc[cells[i]] += summed(Q[second(i)], w, form)

    pipeline(U, lax.div(n - 4 * U + U - 1, U), lambda i: L[cells[i]], operands, *scratch, on_target, on_source)


def own_cells(U, cells, n, table, L, R, Q, acc, scratch):
    def operands(i):
        return jnp.concatenate([R[cells[i]], table[13, 16:32]], 0)

    def on_target(i, w):
        acc[cells[i]] += summed(Q[cells[i]], w)

    pipeline(U, lax.div(n - 4 * U + U - 1, U), lambda i: L[cells[i]], operands, *scratch, None, on_target)


def clear(aimed, gram, weights, turned, wide):
    aimed[...] = jnp.zeros_like(aimed)
    gram[...] = jnp.ones_like(gram)
    weights[...] = jnp.zeros_like(weights)
    turned[...] = jnp.zeros_like(turned)
    wide[...] = jnp.zeros_like(wide)


def start_list(lists, U, values):
    for r, v in zip(lists, values):
        for k in range(4 * U):
            r[k] = v


def list_pair(lists, n, pairs, i, second_base, counts_a, counts_b, half_a, half_b):
    la, lb, lc = lists
    a, b, code = pairs[0, i], pairs[1, i] - second_base, pairs[2, i]
    more_a = (counts_a[a] > CELL).astype(jnp.int32)
    more_b = (counts_b[b] > CELL).astype(jnp.int32)
    for da, db, more in ((0, 0, 1), (half_a, 0, more_a), (0, half_b, more_b), (half_a, half_b, more_a * more_b)):
        la[n] = a + da
        lb[n] = b + db
        lc[n] = code
        n = n + more
    return n


def idle_cell(L, R, Q, at_l, at_r):
    if L is not None:
        L[at_l] = jnp.ones(L.shape[1:], BF16)
    R[at_r] = jnp.zeros(R.shape[1:], BF16)
    Q[at_r] = jnp.zeros(Q.shape[1:], BF16)


def local_kernel(U, V, leaves, slots, npairs, pos, q, counts, pairs, table, shift, acc, L, Q, R, own, half, sizes, stage, la, lb,
                 lc, *scratch):
    dummy = 2 * leaves
    lists = (la, lb, lc)
    acc[...] = jnp.zeros_like(acc)
    idle_cell(L, R, Q, dummy, dummy)
    clear(*scratch)
    start_list((own, half), V, (dummy, dummy))
    start_list(lists, U, (dummy, dummy, 13))
    groups = leaves // 8
    share = npairs // groups

    def extra(g, carry):
        n, nh, nx = carry
        for k in range(8):
            l = 8 * g + k
            more = (counts[l] > CELL).astype(jnp.int32)
            own[n] = l
            own[n + 1] = l + leaves
            half[nh] = l
            n = n + 1 + more
            nh = nh + more
        for k in range(share):
            nx = list_pair(lists, nx, pairs, leaves + g * share + k, 0, counts, counts, leaves, leaves)
        return n, nh, nx

    n, nh, nx = prepare(lambda i, r, s: pos[i, r, s], lambda r, s: q[r, s], leaves, slots, stage, R, Q, L, extra,
                        (4 * V, 4 * V, 4 * U))
    nx = lax.fori_loop(leaves + groups * share, leaves + npairs, lambda i, nx: list_pair(
        lists, nx, pairs, i, 0, counts, counts, leaves, leaves), nx)
    finish_list((own,), n, V, (dummy,))
    finish_list((half,), nh, V, (dummy,))
    finish_list(lists, nx, U, (dummy, dummy, 13))
    sizes[0] = n
    sizes[1] = nh
    cross_cells(U, lists, nx, table, shift, L, Q, acc, R, Q, acc, scratch)


def own_kernel(U, leaves, own, half, sizes, table, L, R, Q, acc_in, acc, *scratch):
    clear(*scratch)
    half_cells(U, leaves, half, sizes[1], table, L, R, Q, acc, scratch)
    clear(*scratch)
    own_cells(U, own, sizes[0], table, L, R, Q, acc, scratch)


def remote_kernel(U, leaves, remotes, slots, npairs, first, rpos, counts, rcounts, pairs, table, shift, L, Qa, acc_in,
                  acc, back, R, Q, acc_b, stage, la, lb, lc, *scratch):
    dummy_a, dummy_b = 2 * leaves, 2 * remotes
    lists = (la, lb, lc)
    acc_b[...] = jnp.zeros_like(acc_b)
    idle_cell(None, R, Q, dummy_a, dummy_b)
    clear(*scratch)
    start_list(lists, U, (dummy_a, dummy_b, 13))
    groups = remotes // 8
    share = npairs // groups

    def extra(g, nx):
        for k in range(share):
            nx = list_pair(lists, nx, pairs, first + g * share + k, leaves, counts, rcounts, leaves, remotes)
        return nx

    nx = prepare(lambda i, r, s: rpos[i, r, s], lambda r, s: rpos[3, r, s], remotes, slots, stage, R, Q, None, extra, 4 * U)
    nx = lax.fori_loop(first + groups * share, first + npairs, lambda i, nx: list_pair(
        lists, nx, pairs, i, leaves, counts, rcounts, leaves, remotes), nx)
    finish_list(lists, nx, U, (dummy_a, dummy_b, 13))
    cross_cells(U, lists, nx, table, shift, L, Qa, acc, R, Q, acc_b, scratch)

    @pl.loop(0, remotes // 8)
    def _(g):
        r = pl.ds(pl.multiple_of(g * 8, 8), 8)
        for h in range(slots // CELL):
            lanes = slice(h * CELL, (h + 1) * CELL)
            cells = pl.ds(pl.multiple_of(h * remotes + g * 8, 8), 8)
            values = finished(acc_b, cells, [rpos[i, r, lanes] for i in range(3)])
            for i in range(4):
                back[i, r, lanes] = values[i]


def finished(acc, cells, pos):
    u = [sum(two_parts(x - 0.5)) for x in pos]
    total = acc[cells, 3, :]
    moments = [acc[cells, i, :] for i in range(3)]
    square = acc[cells, 4, :] + acc[cells, 5, :] + acc[cells, 6, :]
    norm = u[0] * u[0] + u[1] * u[1] + u[2] * u[2]
    dots = u[0] * moments[0] + u[1] * moments[1] + u[2] * moments[2]
    phi = (norm + SOFTEN) * total - 2.0 * dots + square
    return [phi] + [u[i] * total - moments[i] for i in range(3)]


def final_kernel(leaves, remotes, slots, acc, pos, q, occupied, send, back, out):
    @pl.loop(0, leaves // 8)
    def _(g):
        r = pl.ds(pl.multiple_of(g * 8, 8), 8)
        for h in range(slots // CELL):
            lanes = slice(h * CELL, (h + 1) * CELL)
            cells = pl.ds(pl.multiple_of(h * leaves + g * 8, 8), 8)
            values = finished(acc, cells, [pos[i, r, lanes] for i in range(3)])
            values[0] = values[0] - q[r, lanes] * (1.0 / np.sqrt(SOFTEN))
            keep = occupied[r, lanes]
            for i in range(4):
                out[i, r, lanes] = values[i] * keep

    def give(g, _):
        rows = [pl.ds(send[8 * g + k], 1) for k in range(8)]
        keep = [occupied[row, :] for row in rows]
        r = pl.ds(pl.multiple_of(g * 8, 8), 8)
        sums = []
        for i in range(4):
            extra = back[i, r, :]
            sums.append([out[i, rows[k], :] + extra[k : k + 1] * keep[k] for k in range(8)])
        for i in range(4):
            for k in range(8):
                out[i, rows[k], :] = sums[i][k]
        return 0

    lax.fori_loop(0, remotes // 8, give, 0)


SMEM = pl.BlockSpec(memory_space=pltpu.SMEM)
VMEM = pl.BlockSpec(memory_space=pltpu.VMEM)
PARAMS = pltpu.CompilerParams(vmem_limit_bytes=20 << 20)


def scratch_loop(U):
    return [pltpu.VMEM((U, CELL, 32), BF16), pltpu.VMEM((U, CELL, CELL), F32)] + [pltpu.VMEM((U, 2 * CELL, CELL), BF16)] * 2 + [pltpu.VMEM((U, CELL, 2 * CELL), BF16)]


def gather_kernel(remotes, pos, q, counts, send, out):
    lane = lax.broadcasted_iota(jnp.int32, (1, q.shape[1]), 1)

    def body(g, _):
        for k in range(8):
            to, at = pl.ds(8 * g + k, 1), send[8 * g + k]
            row, here = pl.ds(at, 1), lane < counts[at]
            out[0, to, :] = jnp.where(here, pos[0, row, :], 2.0)
            out[1, to, :] = pos[1, row, :]
            out[2, to, :] = pos[2, row, :]
            out[3, to, :] = jnp.where(here, q[row, :], 0.0)
        return 0

    lax.fori_loop(0, remotes // 8, body, 0)


def gather_call(pos, q, counts, send):
    return pl.pallas_call(
        functools.partial(gather_kernel, send.shape[0]),
        out_shape=jax.ShapeDtypeStruct((4, send.shape[0], q.shape[1]), F32),
        in_specs=[VMEM, VMEM, SMEM, SMEM], out_specs=VMEM, compiler_params=PARAMS, name="gather")(pos, q, counts, send)


def pinned(x):
    return pltpu.with_memory_space_constraint(x, pltpu.VMEM)


def local_call(U, V, pos, q, counts, pairs, tables, npairs):
    leaves, slots = q.shape
    cells = 2 * leaves + 1
    room, own_room = (10 + U) * U, (10 + V) * V
    return pl.pallas_call(
        functools.partial(local_kernel, U, V, leaves, slots, npairs),
        out_shape=(pltpu.VMEM((cells, 8, CELL), F32), pltpu.VMEM((cells, 32, CELL), BF16),
                   pltpu.VMEM((cells, 16, CELL), BF16), pltpu.VMEM((cells, 16, CELL), BF16),
                   jax.ShapeDtypeStruct((2 * leaves + own_room,), jnp.int32), jax.ShapeDtypeStruct((leaves + own_room,), jnp.int32),
                   jax.ShapeDtypeStruct((2,), jnp.int32)),
        in_specs=[VMEM, VMEM, SMEM, SMEM, VMEM, VMEM],
        out_specs=(VMEM, VMEM, VMEM, VMEM, SMEM, SMEM, SMEM),
        scratch_shapes=[pltpu.VMEM((2, 5, 64, CELL), F32)]
        + [pltpu.SMEM((4 * npairs + room,), jnp.int32)] * 3 + scratch_loop(U),
        compiler_params=PARAMS, name="local")(pos, q, counts, pairs, *tables)


def remote_call(U, rpos, counts, rcounts, pairs, tables, L, Q, acc, first, npairs):
    leaves = counts.shape[0]
    remotes, slots = rpos.shape[1:]
    cells = 2 * remotes + 1
    return pl.pallas_call(
        functools.partial(remote_kernel, U, leaves, remotes, slots, npairs, first),
        out_shape=(pltpu.VMEM(acc.shape, F32), jax.ShapeDtypeStruct(rpos.shape, F32)),
        in_specs=[VMEM, SMEM, SMEM, SMEM, VMEM, VMEM, VMEM, VMEM, VMEM],
        out_specs=(VMEM, VMEM), input_output_aliases={8: 0},
        scratch_shapes=[pltpu.VMEM((cells, 16, CELL), BF16), pltpu.VMEM((cells, 16, CELL), BF16),
                        pltpu.VMEM((cells, 8, CELL), F32), pltpu.VMEM((2, 4, 64, CELL), F32)]
        + [pltpu.SMEM((4 * npairs + (10 + U) * U,), jnp.int32)] * 3 + scratch_loop(U),
        compiler_params=PARAMS, name="remote")(rpos, counts, rcounts, pairs, *tables, pinned(L), pinned(Q), pinned(acc))


def own_call(U, own, half, sizes, tables, L, R, Q, acc):
    return pl.pallas_call(
        functools.partial(own_kernel, U, (acc.shape[0] - 1) // 2),
        out_shape=pltpu.VMEM(acc.shape, F32),
        in_specs=[SMEM, SMEM, SMEM, VMEM, VMEM, VMEM, VMEM, VMEM],
        out_specs=VMEM, input_output_aliases={7: 0}, scratch_shapes=scratch_loop(U),
        compiler_params=PARAMS, name="own")(own, half, sizes, tables[0], pinned(L), pinned(R), pinned(Q), pinned(acc))


def final_call(acc, pos, q, occupied, send, back):
    leaves, slots = q.shape
    remotes = back.shape[1]
    return pl.pallas_call(
        functools.partial(final_kernel, leaves, remotes, slots),
        out_shape=jax.ShapeDtypeStruct((4, leaves, slots), F32),
        in_specs=[VMEM, VMEM, VMEM, VMEM, SMEM, VMEM], out_specs=VMEM,
        compiler_params=PARAMS, name="final")(pinned(acc), pos, q, occupied, send, back)


def shifted(value, axis, by):
    length = lax.axis_size(axis)
    return lax.ppermute(value, axis, [(i, i + by) for i in range(length) if 0 <= i + by < length])


AXES = ("leaf", "grp")
GROUP, OWN_GROUP = 6, 8


def on_device(positions, charges, counts, send_left, pairs):
    leaves, slots = charges.shape
    remotes = send_left.shape[0]
    near = pairs.shape[1] - leaves - remotes
    remote = shifted(gather_call(positions, charges, counts, send_left), AXES, -1)
    occupied = (jnp.arange(slots)[None, :] < counts[:, None]).astype(jnp.float32)
    charges = charges * occupied
    tables = offset_tables()
    empty = (remote[0, :, CELL] > 1.5) | (lax.axis_index(AXES) == lax.axis_size(AXES) - 1)
    remote_counts = jnp.where(empty, 0, slots).astype(jnp.int32)
    acc, L, Q, R, own, half, sizes = local_call(GROUP, OWN_GROUP, positions, charges, counts, pairs, tables, near)
    acc, back = remote_call(GROUP, remote, counts, remote_counts, pairs, tables, L, Q, acc, leaves + near, remotes)
    returned = shifted(back, AXES, 1)
    acc = own_call(OWN_GROUP, own, half, sizes, tables, L, R, Q, acc)
    return final_call(acc, positions, charges, occupied, send_left, returned)


def solution(mesh):
    in_specs = (P(None, AXES, None), P(AXES, None), P(AXES), P(AXES), P(None, AXES))
    return jax.shard_map(on_device, mesh=mesh, in_specs=in_specs, out_specs=P(None, AXES, None), check_vma=False)
```
